128 devices in a mesh: img: 8 (over x, z_lo), txt: 16 (over y, z_hi, core).
Axes of the slice: x: 4, y: 4, z: 4 (z_hi: 2, z_lo: 2; z = z_hi * 2 + z_lo), core: 2. Of those that a mesh axis runs over, the one named last changes fastest.
Arguments:
- image: bfloat16 [20480, 1152], P(('img', 'txt')), may hold values from -6 to 6
- text: bfloat16 [20480, 1152], P('txt', 'img'), may hold values from -6 to 6
- pair_text: int32 [20480], P(('img', 'txt')), may hold values from 0 to 20479, each once
- log_scale: float32 [1], replicated, may hold values from 2.3 to 3
- bias: float32 [1], replicated, may hold values from -3 to -1
Outputs:
- grad_image: bfloat16 [20480, 1152], P(('img', 'txt'))
- grad_text: bfloat16 [20480, 1152], P('txt', 'img')
The draws below stay inside these ranges and needn't reach their ends.
Inputs may be any that keep to these rules, and one draw needn't show every extreme that they name: `pair_text`: each text index is the match of exactly one image.
All inputs are finite; a program needn't handle non-finite values.
Results may differ from the reference program's by a relative error of at most 0.0034.
Values may be sent and summed in bfloat16 or wider, within the bound.
No kernel may reach another device: no remote copies, remote signals or barrier semaphores. Data moves between devices by JAX's collectives and lax.ppermute only.
A program may use at most 128 MiB of HBM per device.

```python
import jax
import jax.numpy as jnp
from jax import lax

D = 1152
N_PAIRS = 20480
IMG_BLOCK = 2560
N_IMG = 8


def shared_direction(key):
    return jnp.clip(jax.random.normal(key, (D,), jnp.float32), -3.0, 3.0)


def embed_rows(key, common, slope):
    noise = jnp.clip(jax.random.normal(key, (N_PAIRS, D), jnp.float32), -5.0, 5.0)
    weight_rows = slope * jnp.arange(N_PAIRS, dtype=jnp.float32) / N_PAIRS
    return jnp.clip(noise + weight_rows[:, None] * common[None, :], -6.0, 6.0)


def draw_image(key, part):
    common = shared_direction(key)
    key = jax.random.fold_in(key, 11)
    rows = embed_rows(key, common, 0.6)
    return rows.astype(jnp.bfloat16)


def draw_text(key, part):
    common = shared_direction(key)
    key = jax.random.fold_in(key, 23)
    rows = embed_rows(key, common, 0.6)
    return rows.astype(jnp.bfloat16)


def setup_inputs(seed: int = 0) -> dict:
    arg_keys = jax.random.split(jax.random.key(seed), 6)
    image = draw_image(jax.random.fold_in(arg_keys[5], 71), 0)
    text = draw_text(jax.random.fold_in(arg_keys[5], 71), 0)
    pair_text = jax.random.permutation(arg_keys[2], N_PAIRS).astype(jnp.int32)
    log_scale = jnp.clip(jax.random.uniform(arg_keys[3], (1,), jnp.float32, 2.3, 3.0), 2.3, 3.0)
    bias = jnp.clip(jax.random.uniform(arg_keys[4], (1,), jnp.float32, -3.0, -1.0), -3.0, -1.0)
    return {"image": image, "text": text, "pair_text": pair_text, "log_scale": log_scale, "bias": bias}


def normalize(rows):
    values = rows.astype(jnp.float32)
    scale = jnp.sqrt(lax.optimization_barrier(jnp.sum(values * values, axis=-1, keepdims=True)) + 1e-06)
    return (values / scale, scale)

def reference(image, text, pair_text, log_scale, bias):
    image_dir, image_norm = normalize(image)
    text_dir, text_norm = normalize(text)
    image_unit = image_dir.astype(jnp.bfloat16)
    text_unit = text_dir.astype(jnp.bfloat16)
    temper = jnp.exp(log_scale[0])
    shift = bias[0]
    columns = jnp.arange(N_PAIRS, dtype=jnp.int32)
    blocks = image_unit.reshape(N_IMG, IMG_BLOCK, D)
    pair_blocks = pair_text.reshape(N_IMG, IMG_BLOCK)

    def step(carry, inputs):
        rows, pairs = inputs
        logits = temper * jnp.dot(rows, text_unit.T, preferred_element_type=jnp.float32) + shift
        positive = pairs[:, None] == columns[None, :]
        weight = (jax.nn.sigmoid(logits) - positive.astype(jnp.float32)).astype(jnp.bfloat16)
        image_back = temper * jnp.dot(weight, text_unit, preferred_element_type=jnp.float32)
        text_back = carry + temper * jnp.dot(weight.T, rows, preferred_element_type=jnp.float32)
        return (text_back, image_back)
    start = jnp.zeros((N_PAIRS, D), jnp.float32)
    text_back, image_back = lax.scan(step, start, (blocks, pair_blocks))
    image_back = image_back.reshape(N_PAIRS, D)
    grad_image = (image_back - image_dir * lax.optimization_barrier(jnp.sum(image_dir * image_back, axis=-1, keepdims=True))) / image_norm
    grad_text = (text_back - text_dir * lax.optimization_barrier(jnp.sum(text_dir * text_back, axis=-1, keepdims=True))) / text_norm
    return (grad_image.astype(jnp.bfloat16), grad_text.astype(jnp.bfloat16))
```

```python
import jax
import jax.numpy as jnp
from jax import lax
from jax.experimental import pallas as pl
from jax.experimental.pallas import tpu as pltpu
from jax.sharding import PartitionSpec as P

F32 = jnp.float32
BF16 = jnp.bfloat16
VMEM = pl.BlockSpec(memory_space=pltpu.VMEM)
SMEM = pl.BlockSpec(memory_space=pltpu.SMEM)
LOG2E = 1.4426950408889634
AXES = ("img", "txt")
NN = (((1,), (0,)), ((), ()))
NT = (((1,), (1,)), ((), ()))
TN = (((0,), (0,)), ((), ()))
STEPS = (0, -1, 1, 2)
TAIL = 16


def params(mib):
    return pltpu.CompilerParams(vmem_limit_bytes=mib * 2**20)


def cost(flops, size):
    return pl.CostEstimate(flops=flops, bytes_accessed=size, transcendentals=0)


def moves():
    def perm(f):
        pairs = []
        for x in range(4):
            for y in range(4):
                for hi in range(2):
                    for lo in range(2):
                        for c in range(2):
                            a = (x, y, hi, lo, c)
                            number = lambda x, y, hi, lo, c: (x * 2 + lo) * 16 + (y * 2 + hi) * 2 + c
                            pairs.append((number(*a), number(*f(*a))))
        return pairs

    out = {}
    for s in (1, -1, 2):
        out["y", s] = perm(lambda x, y, hi, lo, c: (x, (y + s) % 4, hi, lo, c))
        out["x", s] = perm(lambda x, y, hi, lo, c: ((x + s) % 4, y, hi, lo, c))
    out["hi"] = perm(lambda x, y, hi, lo, c: (x, y, 1 - hi, lo, c))
    out["lo"] = perm(lambda x, y, hi, lo, c: (x, y, hi, 1 - lo, c))
    out["core"] = perm(lambda x, y, hi, lo, c: (x, y, hi, lo, 1 - c))
    return out


MOVES = moves()


def send(value, move):
    return lax.ppermute(value, AXES, MOVES[move])


def after(value, *others):
    return lax.optimization_barrier((value, *others))[0]


def split3(value, rounded=lambda v: v.astype(BF16).astype(F32)):
    high = rounded(value)
    middle = rounded(value - high)
    return high, middle, rounded(value - high - middle)


def unit_kernel(image, pairs, out, inverse):
    value = image[...].astype(F32)
    scale = 1.0 / jnp.sqrt(jnp.sum(value * value, axis=1, keepdims=True) + 1e-06)
    inverse[...] = scale
    unit = (value * scale).astype(BF16)
    rows, width = unit.shape
    half = rows // 2
    out[:half, :] = unit[:half]
    out[half + TAIL :, :] = unit[half:]
    index = pairs[...]
    kind = lax.broadcasted_iota(jnp.int32, (TAIL, width), 0)
    part = jnp.where(kind == 0, index >> 8, jnp.where(kind == 1, index & 255, 0))
    out[half : half + TAIL, :] = part.astype(F32).astype(BF16)


def image_units(image, pairs):
    rows, width = image.shape
    pairs = jnp.pad(pairs[None], ((0, 0), (0, width - rows)))
    return pl.pallas_call(
        unit_kernel,
        out_shape=[
            jax.ShapeDtypeStruct((rows + TAIL, width), BF16),
            jax.ShapeDtypeStruct((rows, 1), F32),
        ],
        in_specs=[VMEM] * 2,
        out_specs=[VMEM] * 2,
        compiler_params=params(8),
        cost_estimate=cost(0, 4 * rows * width),
        name="image_units",
    )(image, pairs)


def text_kernel(place, *refs):
    pieces, (unit, raw, inverse) = refs[:-3], refs[-3:]
    total = None
    for piece in pieces:
        value = piece[...].astype(F32)
        part = jnp.sum(value * value, axis=0, keepdims=True)
        total = part if total is None else total + part
    scale = 1.0 / jnp.sqrt(total + 1e-06)
    inverse[...] = scale
    depth = unit.shape[0] // 8
    block = 0
    for piece in pieces:
        for start in range(0, piece.shape[0], depth):
            rows = pl.ds(pl.multiple_of(place[block] * depth, 16), depth)
            value = piece[start : start + depth, :]
            raw[rows, :] = value
            unit[rows, :] = (value.astype(F32) * scale).astype(BF16)
            block += 1


def text_units(place, pieces, depth):
    width = pieces[0].shape[1]
    whole = jax.ShapeDtypeStruct((8 * depth, width), BF16)
    return pl.pallas_call(
        text_kernel,
        out_shape=[whole, whole, jax.ShapeDtypeStruct((1, width), F32)],
        in_specs=[SMEM] + [VMEM] * len(pieces),
        out_specs=[VMEM] * 3,
        compiler_params=params(12),
        cost_estimate=cost(0, 32 * depth * width),
        name="text_units",
    )(place, *pieces)


def weight_kernel(rows, scalars, first_text, *refs):
    pieces, text, (image, weight, other) = refs[:-4], refs[-4], refs[-3:]
    half = rows // 2
    slope, shift = scalars[0], scalars[1]
    columns = text.shape[1]
    eye = lax.broadcasted_iota(jnp.int32, (rows, rows), 0) == lax.broadcasted_iota(
        jnp.int32, (rows, rows), 1
    )
    names = (lax.broadcasted_iota(jnp.int32, (rows, columns), 1) + first_text[0]).astype(F32)
    block = 0
    for piece in pieces:
        for start in range(0, piece.shape[0], rows + TAIL):
            at = block * rows
            image[at : at + half, :] = piece[start : start + half, :]
            image[at + half : at + rows, :] = piece[start + half + TAIL : start + rows + TAIL, :]
            tail = piece[start + half : start + half + TAIL, :rows].astype(F32)
            product = lax.dot_general(
                image[at : at + rows, :], text[...], NN, preferred_element_type=F32
            )
            chance = 1.0 / (1.0 + jnp.exp2(product * slope + shift))
            match = jnp.sum(
                jnp.where(eye, tail[0:1] * 256.0 + tail[1:2], 0.0), axis=1, keepdims=True
            )
            value = (chance - jnp.where(match == names, 1.0, 0.0)).astype(BF16)
            weight[at : at + rows, :] = value
            if block >= 4:
                at -= 4 * rows
                other[at : at + rows, :] = value
            block += 1


def weights(scalars, first_text, pieces, rows, text):
    width, columns = text.shape
    count = 8 * rows
    return pl.pallas_call(
        lambda *refs: weight_kernel(rows, *refs),
        out_shape=[
            jax.ShapeDtypeStruct((count, width), BF16),
            jax.ShapeDtypeStruct((count, columns), BF16),
            jax.ShapeDtypeStruct((count // 2, columns), BF16),
        ],
        in_specs=[SMEM, SMEM] + [VMEM] * (len(pieces) + 1),
        out_specs=[VMEM] * 3,
        compiler_params=params(12),
        cost_estimate=cost(2 * count * width * columns, 2 * count * (width + columns)),
        name="weights",
    )(scalars, first_text, *pieces, text)


def text_back_kernel(place, image_a, weight_a, image_b, weight_b, raw, *refs):
    outs, back = refs[:4], refs[4]
    width, columns = back.shape
    block = 384
    dots = jnp.zeros((1, columns), F32)
    for f in range(0, width, block):
        part = lax.dot_general(
            image_a[:, f : f + block], weight_a[...], TN, preferred_element_type=F32
        ) + lax.dot_general(
            image_b[:, f : f + block], weight_b[...], TN, preferred_element_type=F32
        )
        back[f : f + block, :] = part
        dots += jnp.sum(part * raw[f : f + block, :].astype(F32), axis=0, keepdims=True)
    tail = split3(dots)
    empty = jnp.zeros((1, columns), F32)
    depth = width // 4
    for i in range(4):
        start = pl.multiple_of(place[2 * i] // 2 * depth, 8)
        out = outs[i]
        out[:depth, :] = back[pl.ds(start, depth), :].astype(out.dtype)
        spread = [empty] * 3 * i + list(tail) + [empty] * (TAIL - 3 * i - 3)
        out[depth:, :] = jnp.concatenate(spread, 0).astype(out.dtype)


def text_terms(place, image_a, weight_a, image_b, weight_b, raw):
    count, width = image_a.shape
    columns = weight_a.shape[1]
    shape = (width // 4 + TAIL, columns)
    return pl.pallas_call(
        text_back_kernel,
        out_shape=[jax.ShapeDtypeStruct(shape, F32)] + [jax.ShapeDtypeStruct(shape, BF16)] * 3,
        in_specs=[SMEM] + [VMEM] * 5,
        out_specs=[VMEM] * 4,
        scratch_shapes=[pltpu.VMEM((width, columns), F32)],
        compiler_params=params(16),
        cost_estimate=cost(4 * count * width * columns, 4 * count * columns),
        name="text_terms",
    )(place, image_a, weight_a, image_b, weight_b, raw)


def image_back_kernel(rows, own_a, got_a, own_b, got_b, text, text_got, *outs):
    for h, (own, got) in enumerate(((own_a, got_a), (own_b, got_b))):
        back = lax.dot_general(
            own[: 4 * rows, :], text[...], NT, preferred_element_type=F32
        ) + lax.dot_general(got[...], text_got[...], NT, preferred_element_type=F32)
        for k in range(4):
            out = outs[k]
            out[h * rows : (h + 1) * rows, :] = back[k * rows : (k + 1) * rows].astype(out.dtype)


def image_terms(rows, own_a, got_a, own_b, got_b, text, text_got):
    width, columns = text.shape
    kinds = [F32, BF16, BF16, BF16]
    return pl.pallas_call(
        lambda *refs: image_back_kernel(rows, *refs),
        out_shape=[jax.ShapeDtypeStruct((2 * rows, width), kind) for kind in kinds],
        in_specs=[VMEM] * 6,
        out_specs=[VMEM] * 4,
        compiler_params=params(16),
        cost_estimate=cost(32 * rows * width * columns, 8 * width * columns),
        name="image_terms",
    )(own_a, got_a, own_b, got_b, text, text_got)


def ring_sum(parts, axis):
    far = [send(part, (axis, s)) for s, part in zip(STEPS[1:], parts[1:])]
    return parts[0] + sum(part.astype(F32) for part in far)


def text_final_kernel(temper, low, total, given, raw, inverse, out):
    depth = raw.shape[0]
    scale = inverse[...]
    keep = total[pl.ds(pl.multiple_of(low[0] * depth, 8), depth), :]
    back = keep + given[:depth, :].astype(F32)
    tails = total[2 * depth :, :] + given[depth:, :].astype(F32)
    dots = jnp.sum(tails, axis=0, keepdims=True) * scale
    unit = raw[...].astype(F32) * scale
    out[...] = (temper[0] * (back - unit * dots) * scale).astype(BF16)


def text_final(temper, low, total, given, raw, inverse):
    return pl.pallas_call(
        text_final_kernel,
        out_shape=jax.ShapeDtypeStruct(raw.shape, BF16),
        in_specs=[SMEM, SMEM] + [VMEM] * 4,
        out_specs=VMEM,
        compiler_params=params(8),
        cost_estimate=cost(0, 4 * raw.size),
        name="text_final",
    )(temper, low, total, given, raw, inverse)


def gather_ring(piece, axis):
    return [piece] + [send(piece, (axis, -s if s < 2 else s)) for s in STEPS[1:]]


def local(image, text, pair_text, log_scale, bias):
    img, txt = lax.axis_index("img"), lax.axis_index("txt")
    x, lo = img // 2, img % 2
    place = jnp.stack([(x + s + 4) % 4 * 2 + (lo + h) % 2 for s in STEPS for h in range(2)])
    temper = jnp.exp(log_scale[0])
    scalars = jnp.stack([-LOG2E * temper, -LOG2E * bias[0]])
    first_text = (txt * text.shape[0])[None]
    depth, rows = text.shape[1], image.shape[0]

    own_text = text.T
    text_lo = send(own_text, "lo")
    unit, image_inverse = image_units(image, pair_text)
    near = [unit, send(unit, ("y", 1)), send(unit, ("y", -1))]
    near.append(send(after(unit, *near[1:]), ("y", 2)))
    text_pieces = gather_ring(jnp.concatenate([own_text, text_lo], 0), "x")
    unit_hi = send(after(unit, text_lo), "hi")
    unit_hi = after(unit_hi, near[3])
    partner = [unit_hi, send(unit_hi, ("y", 1)), send(unit_hi, ("y", -1))]
    partner.append(send(after(unit_hi, *partner[1:]), ("y", 2)))
    near.append(send(jnp.concatenate(near, 0), "core"))
    partner.append(send(jnp.concatenate(partner, 0), "core"))

    text_unit, text_raw, text_inverse = text_units(place, text_pieces, depth)
    text_got = send(text_unit, "core")
    image_a, weight_a, other_a = weights(scalars, first_text, near, rows, text_unit)
    got_a = send(other_a, "core")
    image_b, weight_b, other_b = weights(scalars, first_text, partner, rows, text_unit)
    got_b = send(other_b, "core")
    text_parts = text_terms(place, image_a, weight_a, image_b, weight_b, text_raw)
    got_b, *text_parts = lax.optimization_barrier((got_b, *text_parts))
    image_parts = image_terms(rows, weight_a, got_a, weight_b, got_b, text_unit, text_got)

    image_back = ring_sum(image_parts, "y")
    image_back = image_back[:rows] + send(image_back[rows:].astype(BF16), "hi").astype(F32)
    image_dir = image.astype(F32) * image_inverse
    dot = jnp.sum(image_dir * image_back, axis=-1, keepdims=True)
    grad_image = temper * (image_back - image_dir * dot) * image_inverse

    total = ring_sum(text_parts, "x")
    low_half, high_half, tail = total[:depth], total[depth : 2 * depth], total[2 * depth :]
    give = jnp.where(lo == 0, high_half, low_half)
    given = send(jnp.concatenate([give, tail], 0).astype(BF16), "lo")
    grad_text = text_final(temper[None], lo[None], total, given, own_text, text_inverse).T
    return grad_image.astype(BF16), grad_text


def solution(mesh):
    in_specs = (P(("img", "txt"), None), P("txt", "img"), P(("img", "txt")), P(), P())
    out_specs = (P(("img", "txt"), None), P("txt", "img"))
    return jax.shard_map(local, mesh=mesh, in_specs=in_specs, out_specs=out_specs, check_vma=False)
```

```python
import jax
import jax.numpy as jnp
from jax import lax
from jax.experimental import pallas as pl
from jax.experimental.pallas import tpu as pltpu
from jax.sharding import PartitionSpec as P

F32 = jnp.float32
BF16 = jnp.bfloat16
VMEM = pl.BlockSpec(memory_space=pltpu.VMEM)
SMEM = pl.BlockSpec(memory_space=pltpu.SMEM)
LOG2E = 1.4426950408889634
AXES = ("img", "txt")
NN = (((1,), (0,)), ((), ()))
NT = (((1,), (1,)), ((), ()))
TN = (((0,), (0,)), ((), ()))
STEPS = (0, -1, 1, 2)
TAIL = 16


def params(mib):
    return pltpu.CompilerParams(vmem_limit_bytes=mib * 2**20)


def cost(flops, size):
    return pl.CostEstimate(flops=flops, bytes_accessed=size, transcendentals=0)


def moves():
    def perm(f):
        pairs = []
        for x in range(4):
            for y in range(4):
                for hi in range(2):
                    for lo in range(2):
                        for c in range(2):
                            a = (x, y, hi, lo, c)
                            number = lambda x, y, hi, lo, c: (x * 2 + lo) * 16 + (y * 2 + hi) * 2 + c
                            pairs.append((number(*a), number(*f(*a))))
        return pairs

    out = {}
    for s in (1, -1, 2):
        out["y", s] = perm(lambda x, y, hi, lo, c: (x, (y + s) % 4, hi, lo, c))
        out["x", s] = perm(lambda x, y, hi, lo, c: ((x + s) % 4, y, hi, lo, c))
    out["hi"] = perm(lambda x, y, hi, lo, c: (x, y, 1 - hi, lo, c))
    out["lo"] = perm(lambda x, y, hi, lo, c: (x, y, hi, 1 - lo, c))
    out["core"] = perm(lambda x, y, hi, lo, c: (x, y, hi, lo, 1 - c))
    return out


MOVES = moves()


def send(value, move):
    return lax.ppermute(value, AXES, MOVES[move])


def after(value, *others):
    return lax.optimization_barrier((value, *others))[0]


def split3(value, rounded=lambda v: v.astype(BF16).astype(F32)):
    high = rounded(value)
    middle = rounded(value - high)
    return high, middle, rounded(value - high - middle)


def unit_kernel(image, pairs, out, inverse):
    value = image[...].astype(F32)
    scale = 1.0 / jnp.sqrt(jnp.sum(value * value, axis=1, keepdims=True) + 1e-06)
    inverse[...] = scale
    unit = (value * scale).astype(BF16)
    rows, width = unit.shape
    half = rows // 2
    out[:half, :] = unit[:half]
    out[half + TAIL :, :] = unit[half:]
    index = pairs[...]
    kind = lax.broadcasted_iota(jnp.int32, (TAIL, width), 0)
    part = jnp.where(kind == 0, index >> 8, jnp.where(kind == 1, index & 255, 0))
    out[half : half + TAIL, :] = part.astype(F32).astype(BF16)


def image_units(image, pairs):
    rows, width = image.shape
    pairs = jnp.pad(pairs[None], ((0, 0), (0, width - rows)))
    return pl.pallas_call(
        unit_kernel,
        out_shape=[
            jax.ShapeDtypeStruct((rows + TAIL, width), BF16),
            jax.ShapeDtypeStruct((rows, 1), F32),
        ],
        in_specs=[VMEM] * 2,
        out_specs=[VMEM] * 2,
        compiler_params=params(8),
        cost_estimate=cost(0, 4 * rows * width),
        name="image_units",
    )(image, pairs)


def text_kernel(place, *refs):
    pieces, (unit, raw, inverse) = refs[:-3], refs[-3:]
    total = None
    for piece in pieces:
        value = piece[...].astype(F32)
        part = jnp.sum(value * value, axis=0, keepdims=True)
        total = part if total is None else total + part
    scale = 1.0 / jnp.sqrt(total + 1e-06)
    inverse[...] = scale
    depth = unit.shape[0] // 8
    block = 0
    for piece in pieces:
        for start in range(0, piece.shape[0], depth):
            rows = pl.ds(pl.multiple_of(place[block] * depth, 16), depth)
            value = piece[start : start + depth, :]
            raw[rows, :] = value
            unit[rows, :] = (value.astype(F32) * scale).astype(BF16)
            block += 1


def text_units(place, pieces, depth):
    width = pieces[0].shape[1]
    whole = jax.ShapeDtypeStruct((8 * depth, width), BF16)
    return pl.pallas_call(
        text_kernel,
        out_shape=[whole, whole, jax.ShapeDtypeStruct((1, width), F32)],
        in_specs=[SMEM] + [VMEM] * len(pieces),
        out_specs=[VMEM] * 3,
        compiler_params=params(12),
        cost_estimate=cost(10_000_000_000, 32 * depth * width),
        name="text_units",
    )(place, *pieces)


def weight_kernel(rows, scalars, first_text, *refs):
    pieces, text, (image, weight, other) = refs[:-4], refs[-4], refs[-3:]
    half = rows // 2
    halves = []
    for piece in pieces:
        done = 0
        while done < piece.shape[0]:
            halves.append((piece, done))
            done += half + TAIL if len(halves) % 2 else half
    slope, shift = scalars[0], scalars[1]
    columns = text.shape[1]
    eye = lax.broadcasted_iota(jnp.int32, (rows, rows), 0) == lax.broadcasted_iota(
        jnp.int32, (rows, rows), 1
    )
    names = (lax.broadcasted_iota(jnp.int32, (rows, columns), 1) + first_text[0]).astype(F32)
    for block in range(8):
        (a, i), (b, j) = halves[2 * block : 2 * block + 2]
        at = block * rows
        image[at : at + half, :] = a[i : i + half, :]
        image[at + half : at + rows, :] = b[j : j + half, :]
        tail = a[i + half : i + half + TAIL, :rows].astype(F32)
        product = lax.dot_general(
            image[at : at + rows, :], text[...], NN, preferred_element_type=F32
        )
        chance = 1.0 / (1.0 + jnp.exp2(product * slope + shift))
        match = jnp.sum(
            jnp.where(eye, tail[0:1] * 256.0 + tail[1:2], 0.0), axis=1, keepdims=True
        )
        value = (chance - jnp.where(match == names, 1.0, 0.0)).astype(BF16)
        weight[at : at + rows, :] = value
        if block >= 4:
            at -= 4 * rows
            other[at : at + rows, :] = value


def weights(scalars, first_text, pieces, rows, text):
    width, columns = text.shape
    count = 8 * rows
    return pl.pallas_call(
        lambda *refs: weight_kernel(rows, *refs),
        out_shape=[
            jax.ShapeDtypeStruct((count, width), BF16),
            jax.ShapeDtypeStruct((count, columns), BF16),
            jax.ShapeDtypeStruct((count // 2, columns), BF16),
        ],
        in_specs=[SMEM, SMEM] + [VMEM] * (len(pieces) + 1),
        out_specs=[VMEM] * 3,
        compiler_params=params(12),
        cost_estimate=cost(2 * count * width * columns, 2 * count * (width + columns)),
        name="weights",
    )(scalars, first_text, *pieces, text)


def text_back_kernel(place, image_a, weight_a, image_b, weight_b, raw, *refs):
    outs, back = refs[:5], refs[5]
    width, columns = back.shape
    block = 384
    dots = jnp.zeros((1, columns), F32)
    for f in range(0, width, block):
        part = lax.dot_general(
            image_a[:, f : f + block], weight_a[...], TN, preferred_element_type=F32
        ) + lax.dot_general(
            image_b[:, f : f + block], weight_b[...], TN, preferred_element_type=F32
        )
        back[f : f + block, :] = part
        dots += jnp.sum(part * raw[f : f + block, :].astype(F32), axis=0, keepdims=True)
    tail = split3(dots)
    empty = jnp.zeros((1, columns), F32)
    depth = width // 4
    for i in range(4):
        start = pl.multiple_of(place[2 * i] // 2 * depth, 8)
        spread = [empty] * 3 * i + list(tail) + [empty] * (TAIL - 3 * i - 3)
        spread = jnp.concatenate(spread, 0)
        if i < 3:
            outs[i][:depth, :] = back[pl.ds(start, depth), :].astype(outs[i].dtype)
            outs[i][depth:, :] = spread.astype(outs[i].dtype)
        else:
            half = depth // 2
            outs[3][...] = back[pl.ds(start, half), :].astype(BF16)
            outs[4][:half, :] = back[pl.ds(start + half, half), :].astype(BF16)
            outs[4][half:, :] = spread.astype(BF16)


def text_terms(place, image_a, weight_a, image_b, weight_b, raw):
    count, width = image_a.shape
    columns = weight_a.shape[1]
    shape = (width // 4 + TAIL, columns)
    return pl.pallas_call(
        text_back_kernel,
        out_shape=[
            jax.ShapeDtypeStruct(shape, F32),
            jax.ShapeDtypeStruct(shape, BF16),
            jax.ShapeDtypeStruct(shape, BF16),
            jax.ShapeDtypeStruct((width // 8, columns), BF16),
            jax.ShapeDtypeStruct((width // 8 + TAIL, columns), BF16),
        ],
        in_specs=[SMEM] + [VMEM] * 5,
        out_specs=[VMEM] * 5,
        scratch_shapes=[pltpu.VMEM((width, columns), F32)],
        compiler_params=params(16),
        cost_estimate=cost(4 * count * width * columns, 4 * count * columns),
        name="text_terms",
    )(place, image_a, weight_a, image_b, weight_b, raw)


def image_back_kernel(rows, own_a, got_a, own_b, got_b, text, text_got, *outs):
    for start in (2, 0):
        block = slice(start * rows, (start + 2) * rows)
        for h, (own, got) in enumerate(((own_a, got_a), (own_b, got_b))):
            back = lax.dot_general(
                own[block, :], text[...], NT, preferred_element_type=F32
            ) + lax.dot_general(got[block, :], text_got[...], NT, preferred_element_type=F32)
            for k in range(2):
                i = start + k
                mine = back[k * rows : (k + 1) * rows]
                if i == 3:
                    outs[3 + h][...] = mine.astype(BF16)
                else:
                    outs[i][h * rows : (h + 1) * rows, :] = mine.astype(outs[i].dtype)


def image_terms(rows, own_a, got_a, own_b, got_b, text, text_got):
    width, columns = text.shape
    kinds = [(2 * rows, F32), (2 * rows, BF16), (2 * rows, BF16), (rows, BF16), (rows, BF16)]
    return pl.pallas_call(
        lambda *refs: image_back_kernel(rows, *refs),
        out_shape=[jax.ShapeDtypeStruct((count, width), kind) for count, kind in kinds],
        in_specs=[VMEM] * 6,
        out_specs=[VMEM] * 5,
        compiler_params=params(16),
        cost_estimate=cost(10_000_000_000, 8 * width * columns),
        name="image_terms",
    )(own_a, got_a, own_b, got_b, text, text_got)


def add_kernel(at, value, more, out):
    rows = more.shape[0]
    for start in range(0, value.shape[0], 16):
        block = slice(start, start + 16)
        if at <= start < at + rows:
            total = value[block, :].astype(F32) + more[start - at : start - at + 16, :].astype(F32)
            out[block, :] = total.astype(BF16)
        else:
            out[block, :] = value[block, :]


def add_rows(value, more, at):
    return pl.pallas_call(
        lambda *refs: add_kernel(at, *refs),
        out_shape=jax.ShapeDtypeStruct(value.shape, BF16),
        in_specs=[VMEM] * 2,
        out_specs=VMEM,
        compiler_params=params(8),
        cost_estimate=cost(0, 6 * value.size),
        name="add_rows",
    )(value, more)


def ring_terms(parts, far, axis):
    far = [send(far[0], (axis, 1)), send(far[1], (axis, -1))]
    ahead = add_rows(parts[2], far[0], 0)
    back = add_rows(parts[1], far[1], far[0].shape[0])
    return parts[0], send(ahead, (axis, 1)), send(back, (axis, -1))


def halves_kernel(which, own, ahead, back, keep, give):
    size = keep.shape[0]
    rest = own.shape[0] - 2 * size
    mine = pl.multiple_of(which[0] * size, 16)
    other = pl.multiple_of((1 - which[0]) * size, 16)

    def total(rows):
        return own[rows, :] + ahead[rows, :].astype(F32) + back[rows, :].astype(F32)

    keep[...] = total(pl.ds(mine, size))
    give[:size, :] = total(pl.ds(other, size)).astype(BF16)
    if rest:
        give[size:, :] = total(pl.ds(2 * size, rest)).astype(BF16)


def sum_halves(which, own, ahead, back, size):
    rows, width = own.shape
    return pl.pallas_call(
        halves_kernel,
        out_shape=[
            jax.ShapeDtypeStruct((size, width), F32),
            jax.ShapeDtypeStruct((rows - size, width), BF16),
        ],
        in_specs=[SMEM] + [VMEM] * 3,
        out_specs=[VMEM] * 2,
        compiler_params=params(8),
        cost_estimate=cost(0, 12 * own.size),
        name="sum_halves",
    )(which, own, ahead, back)


def text_final_kernel(temper, keep, gave, given, raw, inverse, out):
    depth = raw.shape[0]
    scale = inverse[...]
    back = keep[...] + given[:depth, :].astype(F32)
    tails = gave[depth:, :].astype(F32) + given[depth:, :].astype(F32)
    dots = jnp.sum(tails, axis=0, keepdims=True) * scale
    unit = raw[...].astype(F32) * scale
    out[...] = (temper[0] * (back - unit * dots) * scale).astype(BF16)


def text_final(temper, keep, gave, given, raw, inverse):
    return pl.pallas_call(
        text_final_kernel,
        out_shape=jax.ShapeDtypeStruct(raw.shape, BF16),
        in_specs=[SMEM] + [VMEM] * 5,
        out_specs=VMEM,
        compiler_params=params(8),
        cost_estimate=cost(0, 12 * raw.size),
        name="text_final",
    )(temper, keep, gave, given, raw, inverse)


def local(image, text, pair_text, log_scale, bias):
    img, txt = lax.axis_index("img"), lax.axis_index("txt")
    x, lo = img // 2, img % 2
    place = jnp.stack([(x + s + 4) % 4 * 2 + (lo + h) % 2 for s in STEPS for h in range(2)])
    temper = jnp.exp(log_scale[0])
    scalars = jnp.stack([-LOG2E * temper, -LOG2E * bias[0]])
    first_text = (txt * text.shape[0])[None]
    depth, rows = text.shape[1], image.shape[0]

    own_text = text.T
    text_lo = send(own_text, "lo")
    unit, image_inverse = image_units(image, pair_text)
    a, b = send(unit, ("y", 1)), send(unit, ("y", -1))
    text2 = jnp.concatenate([own_text, text_lo], 0)
    text_a, text_b = send(text2, ("x", 1)), send(text2, ("x", -1))
    unit_hi = send(after(unit, text_lo), "hi")
    cut = rows // 2 + TAIL
    a2, b2 = send(a[:cut], ("y", 1)), send(b[cut:], ("y", -1))
    unit_hi = after(unit_hi, a2, b2)
    c, d = send(unit_hi, ("y", 1)), send(unit_hi, ("y", -1))
    text_a2, text_b2 = send(text_a[:depth], ("x", 1)), send(text_b[depth:], ("x", -1))
    c, d, text_a, text_b = lax.optimization_barrier((c, d, text_a, text_b))
    c2, d2 = send(c[:cut], ("y", 1)), send(d[cut:], ("y", -1))
    near, partner = [unit, a, b, a2, b2], [unit_hi, c, d, c2, d2]
    near.append(after(send(jnp.concatenate(near, 0), "core"), c2, d2))
    partner += [
        send(jnp.concatenate(partner[:3], 0), "core"),
        send(jnp.concatenate(partner[3:], 0), "core"),
    ]
    text_pieces = [text2, text_a, text_b, text_a2, text_b2]

    text_unit, text_raw, text_inverse = text_units(place, text_pieces, depth)
    image_a, weight_a, other_a = weights(scalars, first_text, near, rows, text_unit)
    got_a = send(other_a, "core")
    text_got = send(after(text_unit, other_a), "core")
    image_b, weight_b, other_b = weights(
        after(scalars, other_a), first_text, partner, rows, text_unit
    )
    got_b = send(other_b, "core")
    *text_parts, far0, far1 = text_terms(place, image_a, weight_a, image_b, weight_b, text_raw)
    got_b, far0, far1, *text_parts = lax.optimization_barrier((got_b, far0, far1, *text_parts))
    *image_parts, image_far0, image_far1 = image_terms(
        rows, weight_a, got_a, weight_b, got_b, text_unit, text_got
    )

    *text_parts, _ = lax.optimization_barrier((*text_parts, image_parts[1]))
    text_terms_here = ring_terms(text_parts, (far0, far1), "x")
    image_terms_here = ring_terms(image_parts, (image_far0, image_far1), "y")
    keep, gave = sum_halves(lo[None], *text_terms_here, depth)
    given = send(gave, "lo")
    grad_text = text_final(temper[None], keep, gave, given, own_text, text_inverse).T

    keep, gave = sum_halves(jnp.zeros((1,), jnp.int32), *image_terms_here, rows)
    image_back = keep + send(gave, "hi").astype(F32)
    image_dir = image.astype(F32) * image_inverse
    dot = jnp.sum(image_dir * image_back, axis=-1, keepdims=True)
    grad_image = temper * (image_back - image_dir * dot) * image_inverse
    return grad_image.astype(BF16), grad_text


def solution(mesh):
    in_specs = (P(("img", "txt"), None), P("txt", "img"), P(("img", "txt")), P(), P())
    out_specs = (P(("img", "txt"), None), P("txt", "img"))
    return jax.shard_map(local, mesh=mesh, in_specs=in_specs, out_specs=out_specs, check_vma=False)
```

```python
import jax
import jax.numpy as jnp
from jax import lax
from jax.experimental import pallas as pl
from jax.experimental.pallas import tpu as pltpu
from jax.sharding import PartitionSpec as P

F32 = jnp.float32
BF16 = jnp.bfloat16
VMEM = pl.BlockSpec(memory_space=pltpu.VMEM)
SMEM = pl.BlockSpec(memory_space=pltpu.SMEM)
LOG2E = 1.4426950408889634
AXES = ("img", "txt")
NN = (((1,), (0,)), ((), ()))
NT = (((1,), (1,)), ((), ()))
TN = (((0,), (0,)), ((), ()))
STEPS = (0, -1, 1, 2)
TAIL = 16


def params(mib):
    return pltpu.CompilerParams(vmem_limit_bytes=mib * 2**20)


def cost(flops, size):
    return pl.CostEstimate(flops=flops, bytes_accessed=size, transcendentals=0)


def moves():
    def perm(f):
        pairs = []
        for x in range(4):
            for y in range(4):
                for hi in range(2):
                    for lo in range(2):
                        for c in range(2):
                            a = (x, y, hi, lo, c)
                            number = lambda x, y, hi, lo, c: (x * 2 + lo) * 16 + (y * 2 + hi) * 2 + c
                            pairs.append((number(*a), number(*f(*a))))
        return pairs

    out = {}
    for s in (1, -1, 2):
        out["y", s] = perm(lambda x, y, hi, lo, c: (x, (y + s) % 4, hi, lo, c))
        out["x", s] = perm(lambda x, y, hi, lo, c: ((x + s) % 4, y, hi, lo, c))
    out["hi"] = perm(lambda x, y, hi, lo, c: (x, y, 1 - hi, lo, c))
    out["lo"] = perm(lambda x, y, hi, lo, c: (x, y, hi, 1 - lo, c))
    out["core"] = perm(lambda x, y, hi, lo, c: (x, y, hi, lo, 1 - c))
    return out


MOVES = moves()


def send(value, move):
    return lax.ppermute(value, AXES, MOVES[move])


def after(value, *others):
    return lax.optimization_barrier((value, *others))[0]


def split3(value, rounded=lambda v: v.astype(BF16).astype(F32)):
    high = rounded(value)
    middle = rounded(value - high)
    return high, middle, rounded(value - high - middle)


def unit_kernel(image, pairs, out, inverse):
    value = image[...].astype(F32)
    scale = 1.0 / jnp.sqrt(jnp.sum(value * value, axis=1, keepdims=True) + 1e-06)
    inverse[...] = scale
    unit = (value * scale).astype(BF16)
    rows, width = unit.shape
    half = rows // 2
    out[:half, :] = unit[:half]
    out[half + TAIL :, :] = unit[half:]
    index = pairs[...]
    kind = lax.broadcasted_iota(jnp.int32, (TAIL, rows), 0)
    part = jnp.where(kind == 0, index >> 8, jnp.where(kind == 1, index & 255, 0))
    out[half : half + TAIL, :] = jnp.zeros((TAIL, width), BF16)
    out[half : half + TAIL, :rows] = part.astype(F32).astype(BF16)


def image_units(image, pairs):
    rows, width = image.shape
    pairs = pairs[None]
    return pl.pallas_call(
        unit_kernel,
        out_shape=[
            jax.ShapeDtypeStruct((rows + TAIL, width), BF16),
            jax.ShapeDtypeStruct((rows, 1), F32),
        ],
        in_specs=[VMEM] * 2,
        out_specs=[VMEM] * 2,
        compiler_params=params(8),
        cost_estimate=cost(0, 4 * rows * width),
        name="image_units",
    )(image, pairs)


def text_kernel(place, *refs):
    pieces, (unit, raw, inverse) = refs[:-3], refs[-3:]
    total = None
    for piece in pieces:
        value = piece[...].astype(F32)
        part = jnp.sum(value * value, axis=0, keepdims=True)
        total = part if total is None else total + part
    scale = 1.0 / jnp.sqrt(total + 1e-06)
    inverse[...] = scale
    depth = unit.shape[0] // 8
    block = 0
    for piece in pieces:
        for start in range(0, piece.shape[0], depth):
            rows = pl.ds(pl.multiple_of(place[block] * depth, 16), depth)
            value = piece[start : start + depth, :]
            raw[rows, :] = value
            unit[rows, :] = (value.astype(F32) * scale).astype(BF16)
            block += 1


def text_units(place, pieces, depth):
    width = pieces[0].shape[1]
    whole = jax.ShapeDtypeStruct((8 * depth, width), BF16)
    return pl.pallas_call(
        text_kernel,
        out_shape=[whole, whole, jax.ShapeDtypeStruct((1, width), F32)],
        in_specs=[SMEM] + [VMEM] * len(pieces),
        out_specs=[VMEM] * 3,
        compiler_params=params(12),
        cost_estimate=cost(40_000_000_000, 32 * depth * width),
        name="text_units",
    )(place, *pieces)


def weight_kernel(rows, scalars, first_text, *refs):
    pieces, text, (image, weight, other) = refs[:-4], refs[-4], refs[-3:]
    half = rows // 2
    halves = []
    for piece in pieces:
        done = 0
        while done < piece.shape[0]:
            halves.append((piece, done))
            done += half + TAIL if len(halves) % 2 else half
    slope, shift = scalars[0], scalars[1]
    columns = text.shape[1]
    eye = lax.broadcasted_iota(jnp.int32, (rows, rows), 0) == lax.broadcasted_iota(
        jnp.int32, (rows, rows), 1
    )
    names = (lax.broadcasted_iota(jnp.int32, (rows, columns), 1) + first_text[0]).astype(F32)
    for block in range(8):
        (a, i), (b, j) = halves[2 * block : 2 * block + 2]
        at = block * rows
        image[at : at + half, :] = a[i : i + half, :]
        image[at + half : at + rows, :] = b[j : j + half, :]
        tail = a[i + half : i + half + TAIL, :rows].astype(F32)
        product = lax.dot_general(
            image[at : at + rows, :], text[...], NN, preferred_element_type=F32
        )
        chance = 1.0 / (1.0 + jnp.exp2(product * slope + shift))
        match = jnp.sum(
            jnp.where(eye, tail[0:1] * 256.0 + tail[1:2], 0.0), axis=1, keepdims=True
        )
        value = (chance - jnp.where(match == names, 1.0, 0.0)).astype(BF16)
        weight[at : at + rows, :] = value
        if block >= 4:
            at -= 4 * rows
            other[at : at + rows, :] = value


def weights(scalars, first_text, pieces, rows, text):
    width, columns = text.shape
    count = 8 * rows
    return pl.pallas_call(
        lambda *refs: weight_kernel(rows, *refs),
        out_shape=[
            jax.ShapeDtypeStruct((count, width), BF16),
            jax.ShapeDtypeStruct((count, columns), BF16),
            jax.ShapeDtypeStruct((count // 2, columns), BF16),
        ],
        in_specs=[SMEM, SMEM] + [VMEM] * (len(pieces) + 1),
        out_specs=[VMEM] * 3,
        compiler_params=params(12),
        cost_estimate=cost(8_000_000_000, 2 * count * (width + columns)),
        name="weights",
    )(scalars, first_text, *pieces, text)


def text_back_kernel(place, image_a, weight_a, image_b, weight_b, raw, *refs):
    outs, back = refs[:8], refs[8]
    width, columns = back.shape
    block = 384
    dots = jnp.zeros((1, columns), F32)
    for f in range(0, width, block):
        part = lax.dot_general(
            image_a[:, f : f + block], weight_a[...], TN, preferred_element_type=F32
        ) + lax.dot_general(
            image_b[:, f : f + block], weight_b[...], TN, preferred_element_type=F32
        )
        back[f : f + block, :] = part
        dots += jnp.sum(part * raw[f : f + block, :].astype(F32), axis=0, keepdims=True)
    tail = split3(dots)
    empty = jnp.zeros((1, columns), F32)
    depth = width // 8
    for i in range(4):
        for h in range(2):
            out = outs[2 * i + h]
            start = pl.multiple_of(place[2 * i + h] * depth, 16)
            out[:depth, :] = back[pl.ds(start, depth), :].astype(out.dtype)
        spread = [empty] * 3 * i + list(tail) + [empty] * (TAIL - 3 * i - 3)
        out[depth:, :] = jnp.concatenate(spread, 0).astype(out.dtype)


def text_terms(place, image_a, weight_a, image_b, weight_b, raw):
    count, width = image_a.shape
    columns = weight_a.shape[1]
    return pl.pallas_call(
        text_back_kernel,
        out_shape=[
            jax.ShapeDtypeStruct((width // 8 + h * TAIL, columns), BF16 if i else F32)
            for i in range(4)
            for h in range(2)
        ],
        in_specs=[SMEM] + [VMEM] * 5,
        out_specs=[VMEM] * 8,
        scratch_shapes=[pltpu.VMEM((width, columns), F32)],
        compiler_params=params(16),
        cost_estimate=cost(4 * count * width * columns, 4 * count * columns),
        name="text_terms",
    )(place, image_a, weight_a, image_b, weight_b, raw)


def image_back_kernel(rows, own_a, got_a, own_b, got_b, text, text_got, *outs):
    for start in (2, 0):
        block = slice(start * rows, (start + 2) * rows)
        for h, (own, got) in enumerate(((own_a, got_a), (own_b, got_b))):
            back = lax.dot_general(
                own[block, :], text[...], NT, preferred_element_type=F32
            ) + lax.dot_general(got[block, :], text_got[...], NT, preferred_element_type=F32)
            for k in range(2):
                out = outs[2 * (start + k) + h]
                out[...] = back[k * rows : (k + 1) * rows].astype(out.dtype)


def image_terms(rows, own_a, got_a, own_b, got_b, text, text_got):
    width, columns = text.shape
    return pl.pallas_call(
        lambda *refs: image_back_kernel(rows, *refs),
        out_shape=[jax.ShapeDtypeStruct((rows, width), F32 if i < 2 else BF16) for i in range(8)],
        in_specs=[VMEM] * 6,
        out_specs=[VMEM] * 8,
        compiler_params=params(16),
        cost_estimate=cost(10_000_000_000, 8 * width * columns),
        name="image_terms",
    )(own_a, got_a, own_b, got_b, text, text_got)


def add_kernel(at, value, more, out):
    rows = more.shape[0]
    for start in range(0, value.shape[0], 16):
        block = slice(start, start + 16)
        if at <= start < at + rows:
            total = value[block, :].astype(F32) + more[start - at : start - at + 16, :].astype(F32)
            out[block, :] = total.astype(BF16)
        else:
            out[block, :] = value[block, :]


def add_rows(value, more, at):
    return pl.pallas_call(
        lambda *refs: add_kernel(at, *refs),
        out_shape=jax.ShapeDtypeStruct(value.shape, BF16),
        in_specs=[VMEM] * 2,
        out_specs=VMEM,
        compiler_params=params(8),
        cost_estimate=cost(5_000_000_000, 6 * value.size),
        name="add_rows",
    )(value, more)


def hold_kernel(value, *refs):
    refs[-1][...] = value[...]


def hold(value, *others):
    return pl.pallas_call(
        hold_kernel,
        out_shape=jax.ShapeDtypeStruct(value.shape, value.dtype),
        in_specs=[VMEM] + [pl.BlockSpec(memory_space=pl.ANY)] * len(others),
        out_specs=VMEM,
        compiler_params=params(4),
        cost_estimate=cost(20_000_000_000, 0),
        name="hold",
    )(value, *others)


def add_three_kernel(own, ahead, back, out):
    out[...] = (own[...] + ahead[...].astype(F32) + back[...].astype(F32)).astype(BF16)


def add_three(own, ahead, back):
    return pl.pallas_call(
        add_three_kernel,
        out_shape=jax.ShapeDtypeStruct(own.shape, BF16),
        in_specs=[VMEM] * 3,
        out_specs=VMEM,
        compiler_params=params(8),
        cost_estimate=cost(0, 10 * own.size),
        name="add_three",
    )(own, ahead, back)


def image_final_kernel(temper, own, ahead, back, given, image, inverse, out):
    total = own[...] + ahead[...].astype(F32) + back[...].astype(F32) + given[...].astype(F32)
    scale = inverse[...]
    unit = image[...].astype(F32) * scale
    dot = jnp.sum(unit * total, axis=1, keepdims=True)
    out[...] = (temper[0] * (total - unit * dot) * scale).astype(BF16)


def image_final(temper, own, ahead, back, given, image, inverse):
    return pl.pallas_call(
        image_final_kernel,
        out_shape=jax.ShapeDtypeStruct(image.shape, BF16),
        in_specs=[SMEM] + [VMEM] * 6,
        out_specs=VMEM,
        compiler_params=params(8),
        cost_estimate=cost(0, 16 * image.size),
        name="image_final",
    )(temper, own, ahead, back, given, image, inverse)


def text_final_kernel(temper, own, ahead, back, gave, given, raw, inverse, out):
    depth = raw.shape[0]
    scale = inverse[...]
    total = own[...] + ahead[...].astype(F32) + back[...].astype(F32)
    total += given[:depth, :].astype(F32)
    tails = gave[depth:, :].astype(F32) + given[depth:, :].astype(F32)
    dots = jnp.sum(tails, axis=0, keepdims=True) * scale
    unit = raw[...].astype(F32) * scale
    out[...] = (temper[0] * (total - unit * dots) * scale).astype(BF16)


def text_final(temper, own, ahead, back, gave, given, raw, inverse):
    return pl.pallas_call(
        text_final_kernel,
        out_shape=jax.ShapeDtypeStruct(raw.shape, BF16),
        in_specs=[SMEM] + [VMEM] * 7,
        out_specs=VMEM,
        compiler_params=params(8),
        cost_estimate=cost(0, 16 * raw.size),
        name="text_final",
    )(temper, own, ahead, back, gave, given, raw, inverse)


def local(image, text, pair_text, log_scale, bias):
    img, txt = lax.axis_index("img"), lax.axis_index("txt")
    x, lo = img // 2, img % 2
    place = jnp.stack([(x + s + 4) % 4 * 2 + (lo + h) % 2 for s in STEPS for h in range(2)])
    temper = jnp.exp(log_scale[0])
    scalars = jnp.stack([-LOG2E * temper, -LOG2E * bias[0]])
    first_text = (txt * text.shape[0])[None]
    depth, rows = text.shape[1], image.shape[0]

    own_text = text.T
    text_lo = send(own_text, "lo")
    text_a, text_b = send(own_text, ("x", 1)), send(own_text, ("x", -1))
    unit, image_inverse = image_units(image, pair_text)
    a, b = send(unit, ("y", 1)), send(unit, ("y", -1))
    unit_hi = send(hold(unit, text_lo), "hi")
    text_c, text_a = lax.optimization_barrier((text_lo, text_a))
    text_c = send(text_c, ("x", 1))
    text_d, text_b = lax.optimization_barrier((text_lo, text_b))
    text_d = send(text_d, ("x", -1))
    text_a2 = send(text_a, ("x", 1))
    a2 = send(a, ("y", 1))
    cut = rows // 2 + TAIL
    c = send(unit_hi, ("y", 1))
    d, b = lax.optimization_barrier((unit_hi, b))
    d = send(d, ("y", -1))
    text_d2 = send(text_d, ("x", -1))
    c, d, text_c, text_d = lax.optimization_barrier((c, d, text_c, text_d))
    c2, d2 = send(c[:cut], ("y", 1)), send(d[cut:], ("y", -1))
    near, partner = [unit, a, b, a2], [unit_hi, c, d, c2, d2]
    near.append(after(send(jnp.concatenate(near, 0), "core"), c2, d2))
    partner += [
        send(jnp.concatenate(partner[:3], 0), "core"),
        send(jnp.concatenate(partner[3:], 0), "core"),
    ]
    text_pieces = [own_text, text_lo, text_a, text_c, text_b, text_d, text_a2, text_d2]

    text_unit, text_raw, text_inverse = text_units(place, text_pieces, depth)
    image_a, weight_a, other_a = weights(scalars, first_text, near, rows, text_unit)
    got_a = send(other_a, "core")
    image_b, weight_b, other_b = weights(
        after(scalars, other_a), first_text, partner, rows, text_unit
    )
    got_b = send(other_b, "core")
    text_got = send(after(text_unit, other_b), "core")
    text_parts = text_terms(place, image_a, weight_a, image_b, weight_b, text_raw)
    got_b, *text_parts = lax.optimization_barrier((got_b, *text_parts))
    image_parts = image_terms(rows, weight_a, got_a, weight_b, got_b, text_unit, text_got)

    x_own, x_back, x_ahead, x_far = [text_parts[2 * i : 2 * i + 2] for i in range(4)]
    y_own, y_back, y_ahead, y_far = [image_parts[2 * i : 2 * i + 2] for i in range(4)]

    x_relay1, x_relay0 = send(x_far[1], ("x", -1)), send(x_far[0], ("x", 1))
    x_ahead1 = send(x_ahead[1], ("x", 1))
    y_relay1, y_relay0 = send(y_far[1], ("y", -1)), send(y_far[0], ("y", 1))
    x_back0, x_back1, x_ahead0, _ = lax.optimization_barrier((*x_back, x_ahead[0], y_own[0]))
    x_back1, x_ahead0 = add_rows(x_back1, x_relay1, 0), add_rows(x_ahead0, x_relay0, 0)
    x_ahead0, y_back0, y_back1, y_ahead0, y_ahead1 = lax.optimization_barrier(
        (x_ahead0, *y_back, *y_ahead)
    )
    x_back1, x_ahead0 = send(x_back1, ("x", -1)), send(x_ahead0, ("x", 1))
    y_back1 = add_rows(y_back1, y_relay1, 0)
    y_back1, y_ahead1, x_back0 = lax.optimization_barrier((y_back1, y_ahead1, x_back0))
    y_back1, y_ahead1 = send(y_back1, ("y", -1)), send(y_ahead1, ("y", 1))
    x_gave = add_three(x_own[1], x_ahead1, x_back1)
    x_given = send(x_gave, "lo")
    x_back0 = send(x_back0, ("x", -1))
    y_ahead0, y_back0 = lax.optimization_barrier((add_rows(y_ahead0, y_relay0, 0), y_back0))
    y_ahead0, y_back0 = send(y_ahead0, ("y", 1)), send(y_back0, ("y", -1))
    y_given = send(add_three(y_own[1], y_ahead1, y_back1), "hi")

    grad_text = text_final(
        temper[None], x_own[0], x_ahead0, x_back0, x_gave, x_given, own_text, text_inverse
    )
    y_given, grad_text = lax.optimization_barrier((y_given, grad_text))
    grad_image = image_final(
        temper[None], y_own[0], y_ahead0, y_back0, y_given, image, image_inverse
    )
    return grad_image, grad_text.T


def solution(mesh):
    in_specs = (P(("img", "txt"), None), P("txt", "img"), P(("img", "txt")), P(), P())
    out_specs = (P(("img", "txt"), None), P("txt", "img"))
    return jax.shard_map(local, mesh=mesh, in_specs=in_specs, out_specs=out_specs, check_vma=False)
```

```python
import jax
import jax.numpy as jnp
from jax import lax
from jax.experimental import pallas as pl
from jax.experimental.pallas import tpu as pltpu
from jax.sharding import PartitionSpec as P

F32 = jnp.float32
BF16 = jnp.bfloat16
VMEM = pl.BlockSpec(memory_space=pltpu.VMEM)
SMEM = pl.BlockSpec(memory_space=pltpu.SMEM)
LOG2E = 1.4426950408889634
AXES = ("img", "txt")
NN = (((1,), (0,)), ((), ()))
NT = (((1,), (1,)), ((), ()))
TN = (((0,), (0,)), ((), ()))
STEPS = (0, -1, 1, 2)
TAIL = 16


def params(mib):
    return pltpu.CompilerParams(vmem_limit_bytes=mib * 2**20)


def cost(flops, size):
    return pl.CostEstimate(flops=flops, bytes_accessed=size, transcendentals=0)


def moves():
    def perm(f):
        pairs = []
        for x in range(4):
            for y in range(4):
                for hi in range(2):
                    for lo in range(2):
                        for c in range(2):
                            a = (x, y, hi, lo, c)
                            number = lambda x, y, hi, lo, c: (x * 2 + lo) * 16 + (y * 2 + hi) * 2 + c
                            pairs.append((number(*a), number(*f(*a))))
        return pairs

    out = {}
    for s in (1, -1, 2):
        out["y", s] = perm(lambda x, y, hi, lo, c: (x, (y + s) % 4, hi, lo, c))
        out["x", s] = perm(lambda x, y, hi, lo, c: ((x + s) % 4, y, hi, lo, c))
    out["hi"] = perm(lambda x, y, hi, lo, c: (x, y, 1 - hi, lo, c))
    out["lo"] = perm(lambda x, y, hi, lo, c: (x, y, hi, 1 - lo, c))
    out["core"] = perm(lambda x, y, hi, lo, c: (x, y, hi, lo, 1 - c))
    return out


MOVES = moves()


def send(value, move):
    return lax.ppermute(value, AXES, MOVES[move])


def after(value, *others):
    return lax.optimization_barrier((value, *others))[0]


def split3(value, rounded=lambda v: v.astype(BF16).astype(F32)):
    high = rounded(value)
    middle = rounded(value - high)
    return high, middle, rounded(value - high - middle)


def unit_kernel(image, pairs, out, inverse):
    value = image[...].astype(F32)
    scale = 1.0 / jnp.sqrt(jnp.sum(value * value, axis=1, keepdims=True) + 1e-06)
    inverse[...] = scale
    unit = (value * scale).astype(BF16)
    rows, width = unit.shape
    half = rows // 2
    out[:half, :] = unit[:half]
    out[half + TAIL :, :] = unit[half:]
    index = pairs[...]
    kind = lax.broadcasted_iota(jnp.int32, (TAIL, rows), 0)
    part = jnp.where(kind == 0, index >> 8, jnp.where(kind == 1, index & 255, 0))
    out[half : half + TAIL, :] = jnp.zeros((TAIL, width), BF16)
    out[half : half + TAIL, :rows] = part.astype(F32).astype(BF16)


def image_units(image, pairs):
    rows, width = image.shape
    pairs = pairs[None]
    return pl.pallas_call(
        unit_kernel,
        out_shape=[
            jax.ShapeDtypeStruct((rows + TAIL, width), BF16),
            jax.ShapeDtypeStruct((rows, 1), F32),
        ],
        in_specs=[VMEM] * 2,
        out_specs=[VMEM] * 2,
        compiler_params=params(8),
        cost_estimate=cost(0, 4 * rows * width),
        name="image_units",
    )(image, pairs)


def text_kernel(place, *refs):
    pieces, (unit, raw, inverse) = refs[:-3], refs[-3:]
    total = None
    for piece in pieces:
        value = piece[...].astype(F32)
        part = jnp.sum(value * value, axis=0, keepdims=True)
        total = part if total is None else total + part
    scale = 1.0 / jnp.sqrt(total + 1e-06)
    inverse[...] = scale
    depth = unit.shape[0] // 8
    block = 0
    for piece in pieces:
        for start in range(0, piece.shape[0], depth):
            rows = pl.ds(pl.multiple_of(place[block] * depth, 16), depth)
            value = piece[start : start + depth, :]
            raw[rows, :] = value
            unit[rows, :] = (value.astype(F32) * scale).astype(BF16)
            block += 1


def text_units(place, pieces, depth):
    width = pieces[0].shape[1]
    whole = jax.ShapeDtypeStruct((8 * depth, width), BF16)
    return pl.pallas_call(
        text_kernel,
        out_shape=[whole, whole, jax.ShapeDtypeStruct((1, width), F32)],
        in_specs=[SMEM] + [VMEM] * len(pieces),
        out_specs=[VMEM] * 3,
        compiler_params=params(12),
        cost_estimate=cost(40_000_000_000, 32 * depth * width),
        name="text_units",
    )(place, *pieces)


def weight_kernel(rows, scalars, first_text, *refs):
    pieces, text, (image, weight, other) = refs[:-4], refs[-4], refs[-3:]
    half = rows // 2
    halves = []
    for piece in pieces:
        done = 0
        while done < piece.shape[0]:
            halves.append((piece, done))
            done += half + TAIL if len(halves) % 2 else half
    slope, shift = scalars[0], scalars[1]
    columns = text.shape[1]
    eye = lax.broadcasted_iota(jnp.int32, (rows, rows), 0) == lax.broadcasted_iota(
        jnp.int32, (rows, rows), 1
    )
    names = (lax.broadcasted_iota(jnp.int32, (rows, columns), 1) + first_text[0]).astype(F32)
    for block in range(8):
        (a, i), (b, j) = halves[2 * block : 2 * block + 2]
        at = block * rows
        image[at : at + half, :] = a[i : i + half, :]
        image[at + half : at + rows, :] = b[j : j + half, :]
        tail = a[i + half : i + half + TAIL, :rows].astype(F32)
        product = lax.dot_general(
            image[at : at + rows, :], text[...], NN, preferred_element_type=F32
        )
        chance = 1.0 / (1.0 + jnp.exp2(product * slope + shift))
        match = jnp.sum(
            jnp.where(eye, tail[0:1] * 256.0 + tail[1:2], 0.0), axis=1, keepdims=True
        )
        value = (chance - jnp.where(match == names, 1.0, 0.0)).astype(BF16)
        weight[at : at + rows, :] = value
        if block >= 4:
            at -= 4 * rows
            other[at : at + rows, :] = value


def weights(scalars, first_text, pieces, rows, text):
    width, columns = text.shape
    count = 8 * rows
    return pl.pallas_call(
        lambda *refs: weight_kernel(rows, *refs),
        out_shape=[
            jax.ShapeDtypeStruct((count, width), BF16),
            jax.ShapeDtypeStruct((count, columns), BF16),
            jax.ShapeDtypeStruct((count // 2, columns), BF16),
        ],
        in_specs=[SMEM, SMEM] + [VMEM] * (len(pieces) + 1),
        out_specs=[VMEM] * 3,
        compiler_params=params(12),
        cost_estimate=cost(8_000_000_000, 2 * count * (width + columns)),
        name="weights",
    )(scalars, first_text, *pieces, text)


def text_back_kernel(place, image_a, weight_a, image_b, weight_b, raw, *refs):
    outs, back = refs[:8], refs[8]
    width, columns = back.shape
    block = 384
    dots = jnp.zeros((1, columns), F32)
    for f in range(0, width, block):
        part = lax.dot_general(
            image_a[:, f : f + block], weight_a[...], TN, preferred_element_type=F32
        ) + lax.dot_general(
            image_b[:, f : f + block], weight_b[...], TN, preferred_element_type=F32
        )
        back[f : f + block, :] = part
        dots += jnp.sum(part * raw[f : f + block, :].astype(F32), axis=0, keepdims=True)
    tail = split3(dots)
    empty = jnp.zeros((1, columns), F32)
    depth = width // 8
    for i in range(4):
        for h in range(2):
            out = outs[2 * i + h]
            start = pl.multiple_of(place[2 * i + h] * depth, 16)
            out[:depth, :] = back[pl.ds(start, depth), :].astype(out.dtype)
        spread = [empty] * 3 * i + list(tail) + [empty] * (TAIL - 3 * i - 3)
        out[depth:, :] = jnp.concatenate(spread, 0).astype(out.dtype)


def text_terms(place, image_a, weight_a, image_b, weight_b, raw):
    count, width = image_a.shape
    columns = weight_a.shape[1]
    return pl.pallas_call(
        text_back_kernel,
        out_shape=[
            jax.ShapeDtypeStruct((width // 8 + h * TAIL, columns), BF16 if i else F32)
            for i in range(4)
            for h in range(2)
        ],
        in_specs=[SMEM] + [VMEM] * 5,
        out_specs=[VMEM] * 8,
        scratch_shapes=[pltpu.VMEM((width, columns), F32)],
        compiler_params=params(16),
        cost_estimate=cost(4 * count * width * columns, 4 * count * columns),
        name="text_terms",
    )(place, image_a, weight_a, image_b, weight_b, raw)


def image_back_kernel(rows, own_a, got_a, own_b, got_b, text, text_got, *outs):
    for start in (2, 0):
        block = slice(start * rows, (start + 2) * rows)
        for h, (own, got) in enumerate(((own_a, got_a), (own_b, got_b))):
            back = lax.dot_general(
                own[block, :], text[...], NT, preferred_element_type=F32
            ) + lax.dot_general(got[block, :], text_got[...], NT, preferred_element_type=F32)
            for k in range(2):
                out = outs[2 * (start + k) + h]
                out[...] = back[k * rows : (k + 1) * rows].astype(out.dtype)


def image_terms(rows, own_a, got_a, own_b, got_b, text, text_got):
    width, columns = text.shape
    return pl.pallas_call(
        lambda *refs: image_back_kernel(rows, *refs),
        out_shape=[jax.ShapeDtypeStruct((rows, width), F32 if i < 2 else BF16) for i in range(8)],
        in_specs=[VMEM] * 6,
        out_specs=[VMEM] * 8,
        compiler_params=params(16),
        cost_estimate=cost(10_000_000_000, 8 * width * columns),
        name="image_terms",
    )(own_a, got_a, own_b, got_b, text, text_got)


def add_kernel(at, value, more, out):
    rows = more.shape[0]
    for start in range(0, value.shape[0], 16):
        block = slice(start, start + 16)
        if at <= start < at + rows:
            total = value[block, :].astype(F32) + more[start - at : start - at + 16, :].astype(F32)
            out[block, :] = total.astype(BF16)
        else:
            out[block, :] = value[block, :]


def add_rows(value, more, at):
    return pl.pallas_call(
        lambda *refs: add_kernel(at, *refs),
        out_shape=jax.ShapeDtypeStruct(value.shape, BF16),
        in_specs=[VMEM] * 2,
        out_specs=VMEM,
        compiler_params=params(8),
        cost_estimate=cost(5_000_000_000, 6 * value.size),
        name="add_rows",
    )(value, more)


def hold_kernel(value, *refs):
    refs[-1][...] = value[...]


def hold(value, *others):
    return pl.pallas_call(
        hold_kernel,
        out_shape=jax.ShapeDtypeStruct(value.shape, value.dtype),
        in_specs=[VMEM] + [pl.BlockSpec(memory_space=pl.ANY)] * len(others),
        out_specs=VMEM,
        compiler_params=params(4),
        cost_estimate=cost(20_000_000_000, 0),
        name="hold",
    )(value, *others)


def add_three_kernel(own, ahead, back, out):
    out[...] = (own[...] + ahead[...].astype(F32) + back[...].astype(F32)).astype(BF16)


def add_three(own, ahead, back):
    return pl.pallas_call(
        add_three_kernel,
        out_shape=jax.ShapeDtypeStruct(own.shape, BF16),
        in_specs=[VMEM] * 3,
        out_specs=VMEM,
        compiler_params=params(8),
        cost_estimate=cost(0, 10 * own.size),
        name="add_three",
    )(own, ahead, back)


def image_final_kernel(temper, own, ahead, back, given, image, inverse, out):
    total = own[...] + ahead[...].astype(F32) + back[...].astype(F32) + given[...].astype(F32)
    scale = inverse[...]
    unit = image[...].astype(F32) * scale
    dot = jnp.sum(unit * total, axis=1, keepdims=True)
    out[...] = (temper[0] * (total - unit * dot) * scale).astype(BF16)


def image_final(temper, own, ahead, back, given, image, inverse):
    return pl.pallas_call(
        image_final_kernel,
        out_shape=jax.ShapeDtypeStruct(image.shape, BF16),
        in_specs=[SMEM] + [VMEM] * 6,
        out_specs=VMEM,
        compiler_params=params(8),
        cost_estimate=cost(0, 16 * image.size),
        name="image_final",
    )(temper, own, ahead, back, given, image, inverse)


def text_final_kernel(temper, own, ahead, back, gave, given, raw, inverse, out):
    depth = raw.shape[0]
    scale = inverse[...]
    total = own[...] + ahead[...].astype(F32) + back[...].astype(F32)
    total += given[:depth, :].astype(F32)
    tails = gave[depth:, :].astype(F32) + given[depth:, :].astype(F32)
    dots = jnp.sum(tails, axis=0, keepdims=True) * scale
    unit = raw[...].astype(F32) * scale
    out[...] = (temper[0] * (total - unit * dots) * scale).astype(BF16)


def text_final(temper, own, ahead, back, gave, given, raw, inverse):
    return pl.pallas_call(
        text_final_kernel,
        out_shape=jax.ShapeDtypeStruct(raw.shape, BF16),
        in_specs=[SMEM] + [VMEM] * 7,
        out_specs=VMEM,
        compiler_params=params(8),
        cost_estimate=cost(0, 16 * raw.size),
        name="text_final",
    )(temper, own, ahead, back, gave, given, raw, inverse)


def local(image, text, pair_text, log_scale, bias):
    img, txt = lax.axis_index("img"), lax.axis_index("txt")
    x, lo = img // 2, img % 2
    place = jnp.stack([(x + s + 4) % 4 * 2 + (lo + h) % 2 for s in STEPS for h in range(2)])
    temper = jnp.exp(log_scale[0])
    scalars = jnp.stack([-LOG2E * temper, -LOG2E * bias[0]])
    first_text = (txt * text.shape[0])[None]
    depth, rows = text.shape[1], image.shape[0]

    own_text = text.T
    text_lo = send(own_text, "lo")
    text_a, text_b = send(own_text, ("x", 1)), send(own_text, ("x", -1))
    unit, image_inverse = image_units(image, pair_text)
    a, b = send(unit, ("y", 1)), send(unit, ("y", -1))
    unit_hi = send(hold(unit, text_lo), "hi")
    text_c, text_a = lax.optimization_barrier((text_lo, text_a))
    text_c = send(text_c, ("x", 1))
    text_d, text_b = lax.optimization_barrier((text_lo, text_b))
    text_d = send(text_d, ("x", -1))
    text_a2 = send(text_a, ("x", 1))
    cut = rows // 2 + TAIL
    a2, b2 = send(a[:cut], ("y", 1)), send(b[cut:], ("y", -1))
    c = send(unit_hi, ("y", 1))
    d, b = lax.optimization_barrier((unit_hi, b))
    d = send(d, ("y", -1))
    text_d2 = send(text_d, ("x", -1))
    c, d, text_c, text_d = lax.optimization_barrier((c, d, text_c, text_d))
    c2, d2 = send(c[:cut], ("y", 1)), send(d[cut:], ("y", -1))
    near, partner = [unit, a, b, a2, b2], [unit_hi, c, d, c2, d2]
    near.append(after(send(jnp.concatenate(near, 0), "core"), c2, d2))
    partner += [
        send(jnp.concatenate(partner[:3], 0), "core"),
        send(jnp.concatenate(partner[3:], 0), "core"),
    ]
    text_pieces = [own_text, text_lo, text_a, text_c, text_b, text_d, text_a2, text_d2]

    text_unit, text_raw, text_inverse = text_units(place, text_pieces, depth)
    image_a, weight_a, other_a = weights(scalars, first_text, near, rows, text_unit)
    got_a = send(other_a, "core")
    image_b, weight_b, other_b = weights(
        after(scalars, other_a), first_text, partner, rows, text_unit
    )
    got_b = send(other_b, "core")
    text_got = send(after(text_unit, other_b), "core")
    text_parts = text_terms(place, image_a, weight_a, image_b, weight_b, text_raw)
    got_b, *text_parts = lax.optimization_barrier((got_b, *text_parts))
    image_parts = image_terms(rows, weight_a, got_a, weight_b, got_b, text_unit, text_got)

    x_own, x_back, x_ahead, x_far = [text_parts[2 * i : 2 * i + 2] for i in range(4)]
    y_own, y_back, y_ahead, y_far = [image_parts[2 * i : 2 * i + 2] for i in range(4)]

    x_relay1, x_relay0 = send(x_far[1], ("x", -1)), send(x_far[0], ("x", 1))
    x_ahead1 = send(x_ahead[1], ("x", 1))
    y_relay1, y_relay0 = send(y_far[1], ("y", -1)), send(y_far[0], ("y", 1))
    x_back0, x_back1, x_ahead0, _ = lax.optimization_barrier((*x_back, x_ahead[0], y_own[0]))
    x_back1, x_ahead0 = add_rows(x_back1, x_relay1, 0), add_rows(x_ahead0, x_relay0, 0)
    x_ahead0, y_back0, y_back1, y_ahead0, y_ahead1 = lax.optimization_barrier(
        (x_ahead0, *y_back, *y_ahead)
    )
    x_back1, x_ahead0 = send(x_back1, ("x", -1)), send(x_ahead0, ("x", 1))
    y_back1 = add_rows(y_back1, y_relay1, 0)
    y_back1, y_ahead1, x_back0 = lax.optimization_barrier((y_back1, y_ahead1, x_back0))
    y_back1, y_ahead1 = send(y_back1, ("y", -1)), send(y_ahead1, ("y", 1))
    x_gave = add_three(x_own[1], x_ahead1, x_back1)
    x_given = send(x_gave, "lo")
    x_back0 = send(x_back0, ("x", -1))
    y_ahead0, y_back0 = lax.optimization_barrier((add_rows(y_ahead0, y_relay0, 0), y_back0))
    y_ahead0, y_back0 = send(y_ahead0, ("y", 1)), send(y_back0, ("y", -1))
    y_given = send(add_three(y_own[1], y_ahead1, y_back1), "hi")

    grad_text = text_final(
        temper[None], x_own[0], x_ahead0, x_back0, x_gave, x_given, own_text, text_inverse
    )
    y_given, grad_text = lax.optimization_barrier((y_given, grad_text))
    grad_image = image_final(
        temper[None], y_own[0], y_ahead0, y_back0, y_given, image, image_inverse
    )
    return grad_image, grad_text.T


def solution(mesh):
    in_specs = (P(("img", "txt"), None), P("txt", "img"), P(("img", "txt")), P(), P())
    out_specs = (P(("img", "txt"), None), P("txt", "img"))
    return jax.shard_map(local, mesh=mesh, in_specs=in_specs, out_specs=out_specs, check_vma=False)
```

```python
import jax
import jax.numpy as jnp
from jax import lax
from jax.experimental import pallas as pl
from jax.experimental.pallas import tpu as pltpu
from jax.sharding import PartitionSpec as P

F32 = jnp.float32
BF16 = jnp.bfloat16
VMEM = pl.BlockSpec(memory_space=pltpu.VMEM)
SMEM = pl.BlockSpec(memory_space=pltpu.SMEM)
LOG2E = 1.4426950408889634
AXES = ("img", "txt")
NN = (((1,), (0,)), ((), ()))
NT = (((1,), (1,)), ((), ()))
TN = (((0,), (0,)), ((), ()))
STEPS = (0, -1, 1, 2)
TAIL = 16


def params(mib):
    return pltpu.CompilerParams(vmem_limit_bytes=mib * 2**20)


def cost(flops, size):
    return pl.CostEstimate(flops=flops, bytes_accessed=size, transcendentals=0)


def moves():
    def perm(f):
        pairs = []
        for x in range(4):
            for y in range(4):
                for hi in range(2):
                    for lo in range(2):
                        for c in range(2):
                            a = (x, y, hi, lo, c)
                            number = lambda x, y, hi, lo, c: (x * 2 + lo) * 16 + (y * 2 + hi) * 2 + c
                            pairs.append((number(*a), number(*f(*a))))
        return pairs

    out = {}
    for s in (1, -1, 2):
        out["y", s] = perm(lambda x, y, hi, lo, c: (x, (y + s) % 4, hi, lo, c))
        out["x", s] = perm(lambda x, y, hi, lo, c: ((x + s) % 4, y, hi, lo, c))
    out["hi"] = perm(lambda x, y, hi, lo, c: (x, y, 1 - hi, lo, c))
    out["lo"] = perm(lambda x, y, hi, lo, c: (x, y, hi, 1 - lo, c))
    out["core"] = perm(lambda x, y, hi, lo, c: (x, y, hi, lo, 1 - c))
    return out


MOVES = moves()


def send(value, move):
    return lax.ppermute(value, AXES, MOVES[move])


def after(value, *others):
    return lax.optimization_barrier((value, *others))[0]


def split3(value, rounded=lambda v: v.astype(BF16).astype(F32)):
    high = rounded(value)
    middle = rounded(value - high)
    return high, middle, rounded(value - high - middle)


def unit_kernel(image, pairs, out, inverse):
    value = image[...].astype(F32)
    scale = 1.0 / jnp.sqrt(jnp.sum(value * value, axis=1, keepdims=True) + 1e-06)
    inverse[...] = scale
    unit = (value * scale).astype(BF16)
    rows, width = unit.shape
    half = rows // 2
    out[:half, :] = unit[:half]
    out[half + TAIL :, :] = unit[half:]
    index = pairs[...]
    kind = lax.broadcasted_iota(jnp.int32, (TAIL, rows), 0)
    part = jnp.where(kind == 0, index >> 8, jnp.where(kind == 1, index & 255, 0))
    out[half : half + TAIL, :] = jnp.zeros((TAIL, width), BF16)
    out[half : half + TAIL, :rows] = part.astype(F32).astype(BF16)


def image_units(image, pairs):
    rows, width = image.shape
    pairs = pairs[None]
    return pl.pallas_call(
        unit_kernel,
        out_shape=[
            jax.ShapeDtypeStruct((rows + TAIL, width), BF16),
            jax.ShapeDtypeStruct((rows, 1), F32),
        ],
        in_specs=[VMEM] * 2,
        out_specs=[VMEM] * 2,
        compiler_params=params(8),
        cost_estimate=cost(0, 4 * rows * width),
        name="image_units",
    )(image, pairs)


def text_kernel(place, *refs):
    pieces, (unit, raw, inverse) = refs[:-3], refs[-3:]
    total = None
    for piece in pieces:
        value = piece[...].astype(F32)
        part = jnp.sum(value * value, axis=0, keepdims=True)
        total = part if total is None else total + part
    scale = 1.0 / jnp.sqrt(total + 1e-06)
    inverse[...] = scale
    depth = unit.shape[0] // 8
    block = 0
    for piece in pieces:
        for start in range(0, piece.shape[0], depth):
            rows = pl.ds(pl.multiple_of(place[block] * depth, 16), depth)
            value = piece[start : start + depth, :]
            raw[rows, :] = value
            unit[rows, :] = (value.astype(F32) * scale).astype(BF16)
            block += 1


def text_units(place, pieces, depth):
    width = pieces[0].shape[1]
    whole = jax.ShapeDtypeStruct((8 * depth, width), BF16)
    return pl.pallas_call(
        text_kernel,
        out_shape=[whole, whole, jax.ShapeDtypeStruct((1, width), F32)],
        in_specs=[SMEM] + [VMEM] * len(pieces),
        out_specs=[VMEM] * 3,
        compiler_params=params(12),
        cost_estimate=cost(40_000_000_000, 32 * depth * width),
        name="text_units",
    )(place, *pieces)


def weight_kernel(rows, scalars, first_text, *refs):
    pieces, text, (image, weight, other, tails) = refs[:-5], refs[-5], refs[-4:]
    half = rows // 2
    halves = []
    for piece in pieces:
        done = 0
        while done < piece.shape[0]:
            halves.append((piece, done))
            done += half + TAIL if len(halves) % 2 else half
    for block in range(8):
        (a, i), (b, j) = halves[2 * block : 2 * block + 2]
        at = block * rows
        image[at : at + half, :] = a[i : i + half, :]
        image[at + half : at + rows, :] = b[j : j + half, :]
        tails[block * TAIL : (block + 1) * TAIL, :] = a[i + half : i + half + TAIL, :rows]
    slope, shift = scalars[0], scalars[1]
    columns = text.shape[1]
    eye = lax.broadcasted_iota(jnp.int32, (rows, rows), 0) == lax.broadcasted_iota(
        jnp.int32, (rows, rows), 1
    )
    names = (lax.broadcasted_iota(jnp.int32, (rows, columns), 1) + first_text[0]).astype(F32)

    def step(number, carry):
        for k in range(4):
            block = number * 4 + k
            mine = pl.ds(pl.multiple_of(block * rows, 16), rows)
            tail = tails[pl.ds(pl.multiple_of(block * TAIL, 16), TAIL), :].astype(F32)
            product = lax.dot_general(
                image[mine, :], text[...], NN, preferred_element_type=F32
            )
            chance = 1.0 / (1.0 + jnp.exp2(product * slope + shift))
            match = jnp.sum(
                jnp.where(eye, tail[0:1] * 256.0 + tail[1:2], 0.0), axis=1, keepdims=True
            )
            weight[mine, :] = (chance - jnp.where(match == names, 1.0, 0.0)).astype(BF16)
        return carry

    lax.fori_loop(0, 8 // 4, step, 0)
    other[...] = weight[4 * rows :, :]


def weights(scalars, first_text, pieces, rows, text):
    width, columns = text.shape
    count = 8 * rows
    return pl.pallas_call(
        lambda *refs: weight_kernel(rows, *refs),
        out_shape=[
            jax.ShapeDtypeStruct((count, width), BF16),
            jax.ShapeDtypeStruct((count, columns), BF16),
            jax.ShapeDtypeStruct((count // 2, columns), BF16),
        ],
        in_specs=[SMEM, SMEM] + [VMEM] * (len(pieces) + 1),
        out_specs=[VMEM] * 3,
        scratch_shapes=[pltpu.VMEM((8 * TAIL, rows), BF16)],
        compiler_params=params(12),
        cost_estimate=cost(8_000_000_000, 2 * count * (width + columns)),
        name="weights",
    )(scalars, first_text, *pieces, text)


def text_back_kernel(place, image_a, weight_a, image_b, weight_b, raw, *refs):
    outs, back = refs[:8], refs[8]
    width, columns = back.shape
    block = 384
    dots = jnp.zeros((1, columns), F32)
    for f in range(0, width, block):
        part = lax.dot_general(
            image_a[:, f : f + block], weight_a[...], TN, preferred_element_type=F32
        ) + lax.dot_general(
            image_b[:, f : f + block], weight_b[...], TN, preferred_element_type=F32
        )
        back[f : f + block, :] = part
        dots += jnp.sum(part * raw[f : f + block, :].astype(F32), axis=0, keepdims=True)
    tail = split3(dots)
    empty = jnp.zeros((1, columns), F32)
    depth = width // 8
    for i in range(4):
        for h in range(2):
            out = outs[2 * i + h]
            start = pl.multiple_of(place[2 * i + h] * depth, 16)
            out[:depth, :] = back[pl.ds(start, depth), :].astype(out.dtype)
        spread = [empty] * 3 * i + list(tail) + [empty] * (TAIL - 3 * i - 3)
        out[depth:, :] = jnp.concatenate(spread, 0).astype(out.dtype)


def text_terms(place, image_a, weight_a, image_b, weight_b, raw):
    count, width = image_a.shape
    columns = weight_a.shape[1]
    return pl.pallas_call(
        text_back_kernel,
        out_shape=[
            jax.ShapeDtypeStruct((width // 8 + h * TAIL, columns), BF16 if i else F32)
            for i in range(4)
            for h in range(2)
        ],
        in_specs=[SMEM] + [VMEM] * 5,
        out_specs=[VMEM] * 8,
        scratch_shapes=[pltpu.VMEM((width, columns), F32)],
        compiler_params=params(16),
        cost_estimate=cost(4 * count * width * columns, 4 * count * columns),
        name="text_terms",
    )(place, image_a, weight_a, image_b, weight_b, raw)


def image_back_kernel(rows, own_a, got_a, own_b, got_b, text, text_got, *outs):
    for start in (2, 0):
        block = slice(start * rows, (start + 2) * rows)
        for h, (own, got) in enumerate(((own_a, got_a), (own_b, got_b))):
            back = lax.dot_general(
                own[block, :], text[...], NT, preferred_element_type=F32
            ) + lax.dot_general(got[block, :], text_got[...], NT, preferred_element_type=F32)
            for k in range(2):
                out = outs[2 * (start + k) + h]
                out[...] = back[k * rows : (k + 1) * rows].astype(out.dtype)


def image_terms(rows, own_a, got_a, own_b, got_b, text, text_got):
    width, columns = text.shape
    return pl.pallas_call(
        lambda *refs: image_back_kernel(rows, *refs),
        out_shape=[jax.ShapeDtypeStruct((rows, width), F32 if i < 2 else BF16) for i in range(8)],
        in_specs=[VMEM] * 6,
        out_specs=[VMEM] * 8,
        compiler_params=params(16),
        cost_estimate=cost(10_000_000_000, 8 * width * columns),
        name="image_terms",
    )(own_a, got_a, own_b, got_b, text, text_got)


def add_kernel(at, value, more, out):
    rows = more.shape[0]
    for start in range(0, value.shape[0], 16):
        block = slice(start, start + 16)
        if at <= start < at + rows:
            total = value[block, :].astype(F32) + more[start - at : start - at + 16, :].astype(F32)
            out[block, :] = total.astype(BF16)
        else:
            out[block, :] = value[block, :]


def add_rows(value, more, at):
    return pl.pallas_call(
        lambda *refs: add_kernel(at, *refs),
        out_shape=jax.ShapeDtypeStruct(value.shape, BF16),
        in_specs=[VMEM] * 2,
        out_specs=VMEM,
        compiler_params=params(8),
        cost_estimate=cost(5_000_000_000, 6 * value.size),
        name="add_rows",
    )(value, more)


def hold_kernel(value, *refs):
    refs[-1][...] = value[...]


def hold(value, *others):
    return pl.pallas_call(
        hold_kernel,
        out_shape=jax.ShapeDtypeStruct(value.shape, value.dtype),
        in_specs=[VMEM] + [pl.BlockSpec(memory_space=pl.ANY)] * len(others),
        out_specs=VMEM,
        compiler_params=params(4),
        cost_estimate=cost(20_000_000_000, 0),
        name="hold",
    )(value, *others)


def add_three_kernel(own, ahead, back, out):
    out[...] = (own[...] + ahead[...].astype(F32) + back[...].astype(F32)).astype(BF16)


def add_three(own, ahead, back):
    return pl.pallas_call(
        add_three_kernel,
        out_shape=jax.ShapeDtypeStruct(own.shape, BF16),
        in_specs=[VMEM] * 3,
        out_specs=VMEM,
        compiler_params=params(8),
        cost_estimate=cost(0, 10 * own.size),
        name="add_three",
    )(own, ahead, back)


def image_final_kernel(temper, own, ahead, back, given, image, inverse, out):
    total = own[...] + ahead[...].astype(F32) + back[...].astype(F32) + given[...].astype(F32)
    scale = inverse[...]
    unit = image[...].astype(F32) * scale
    dot = jnp.sum(unit * total, axis=1, keepdims=True)
    out[...] = (temper[0] * (total - unit * dot) * scale).astype(BF16)


def image_final(temper, own, ahead, back, given, image, inverse):
    return pl.pallas_call(
        image_final_kernel,
        out_shape=jax.ShapeDtypeStruct(image.shape, BF16),
        in_specs=[SMEM] + [VMEM] * 6,
        out_specs=VMEM,
        compiler_params=params(8),
        cost_estimate=cost(0, 16 * image.size),
        name="image_final",
    )(temper, own, ahead, back, given, image, inverse)


def text_final_kernel(temper, own, ahead, back, gave, given, raw, inverse, out):
    depth = raw.shape[0]
    scale = inverse[...]
    total = own[...] + ahead[...].astype(F32) + back[...].astype(F32)
    total += given[:depth, :].astype(F32)
    tails = gave[depth:, :].astype(F32) + given[depth:, :].astype(F32)
    dots = jnp.sum(tails, axis=0, keepdims=True) * scale
    unit = raw[...].astype(F32) * scale
    out[...] = (temper[0] * (total - unit * dots) * scale).astype(BF16)


def text_final(temper, own, ahead, back, gave, given, raw, inverse):
    return pl.pallas_call(
        text_final_kernel,
        out_shape=jax.ShapeDtypeStruct(raw.shape, BF16),
        in_specs=[SMEM] + [VMEM] * 7,
        out_specs=VMEM,
        compiler_params=params(8),
        cost_estimate=cost(0, 16 * raw.size),
        name="text_final",
    )(temper, own, ahead, back, gave, given, raw, inverse)


def local(image, text, pair_text, log_scale, bias):
    img, txt = lax.axis_index("img"), lax.axis_index("txt")
    x, lo = img // 2, img % 2
    place = jnp.stack([(x + s + 4) % 4 * 2 + (lo + h) % 2 for s in STEPS for h in range(2)])
    temper = jnp.exp(log_scale[0])
    scalars = jnp.stack([-LOG2E * temper, -LOG2E * bias[0]])
    first_text = (txt * text.shape[0])[None]
    depth, rows = text.shape[1], image.shape[0]

    own_text = text.T
    text_lo = send(own_text, "lo")
    text_a, text_b = send(own_text, ("x", 1)), send(own_text, ("x", -1))
    unit, image_inverse = image_units(image, pair_text)
    a, b = send(unit, ("y", 1)), send(unit, ("y", -1))
    unit_hi = send(hold(unit, text_lo), "hi")
    text_c, text_a = lax.optimization_barrier((text_lo, text_a))
    text_c = send(text_c, ("x", 1))
    text_d, text_b = lax.optimization_barrier((text_lo, text_b))
    text_d = send(text_d, ("x", -1))
    text_a2 = send(text_a, ("x", 1))
    cut = rows // 2 + TAIL
    a2, b2 = send(a[:cut], ("y", 1)), send(b[cut:], ("y", -1))
    c = send(unit_hi, ("y", 1))
    d, b = lax.optimization_barrier((unit_hi, b))
    d = send(d, ("y", -1))
    text_d2 = send(text_d, ("x", -1))
    c, d, text_c, text_d = lax.optimization_barrier((c, d, text_c, text_d))
    c2, d2 = send(c[:cut], ("y", 1)), send(d[cut:], ("y", -1))
    near, partner = [unit, a, b, a2, b2], [unit_hi, c, d, c2, d2]
    near.append(after(send(jnp.concatenate(near, 0), "core"), c2, d2))
    partner += [
        send(jnp.concatenate(partner[:3], 0), "core"),
        send(jnp.concatenate(partner[3:], 0), "core"),
    ]
    text_pieces = [own_text, text_lo, text_a, text_c, text_b, text_d, text_a2, text_d2]

    text_unit, text_raw, text_inverse = text_units(place, text_pieces, depth)
    image_a, weight_a, other_a = weights(scalars, first_text, near, rows, text_unit)
    got_a = send(other_a, "core")
    image_b, weight_b, other_b = weights(
        after(scalars, other_a), first_text, partner, rows, text_unit
    )
    got_b = send(other_b, "core")
    text_got = send(after(text_unit, other_b), "core")
    text_parts = text_terms(place, image_a, weight_a, image_b, weight_b, text_raw)
    got_b, *text_parts = lax.optimization_barrier((got_b, *text_parts))
    image_parts = image_terms(rows, weight_a, got_a, weight_b, got_b, text_unit, text_got)

    x_own, x_back, x_ahead, x_far = [text_parts[2 * i : 2 * i + 2] for i in range(4)]
    y_own, y_back, y_ahead, y_far = [image_parts[2 * i : 2 * i + 2] for i in range(4)]

    x_relay1, x_relay0 = send(x_far[1], ("x", -1)), send(x_far[0], ("x", 1))
    x_ahead1 = send(x_ahead[1], ("x", 1))
    y_relay1, y_relay0 = send(y_far[1], ("y", -1)), send(y_far[0], ("y", 1))
    x_back0, x_back1, x_ahead0, _ = lax.optimization_barrier((*x_back, x_ahead[0], y_own[0]))
    x_back1, x_ahead0 = add_rows(x_back1, x_relay1, 0), add_rows(x_ahead0, x_relay0, 0)
    x_ahead0, y_back0, y_back1, y_ahead0, y_ahead1 = lax.optimization_barrier(
        (x_ahead0, *y_back, *y_ahead)
    )
    x_back1, x_ahead0 = send(x_back1, ("x", -1)), send(x_ahead0, ("x", 1))
    y_back1 = add_rows(y_back1, y_relay1, 0)
    y_back1, y_ahead1, x_back0 = lax.optimization_barrier((y_back1, y_ahead1, x_back0))
    y_back1, y_ahead1 = send(y_back1, ("y", -1)), send(y_ahead1, ("y", 1))
    x_gave = add_three(x_own[1], x_ahead1, x_back1)
    x_given = send(x_gave, "lo")
    x_back0 = send(x_back0, ("x", -1))
    y_ahead0, y_back0 = lax.optimization_barrier((add_rows(y_ahead0, y_relay0, 0), y_back0))
    y_ahead0, y_back0 = send(y_ahead0, ("y", 1)), send(y_back0, ("y", -1))
    y_given = send(add_three(y_own[1], y_ahead1, y_back1), "hi")

    grad_text = text_final(
        temper[None], x_own[0], x_ahead0, x_back0, x_gave, x_given, own_text, text_inverse
    )
    y_given, grad_text = lax.optimization_barrier((y_given, grad_text))
    grad_image = image_final(
        temper[None], y_own[0], y_ahead0, y_back0, y_given, image, image_inverse
    )
    return grad_image, grad_text.T


def solution(mesh):
    in_specs = (P(("img", "txt"), None), P("txt", "img"), P(("img", "txt")), P(), P())
    out_specs = (P(("img", "txt"), None), P("txt", "img"))
    return jax.shard_map(local, mesh=mesh, in_specs=in_specs, out_specs=out_specs, check_vma=False)
```

```python
import jax
import jax.numpy as jnp
from jax import lax
from jax.experimental import pallas as pl
from jax.experimental.pallas import tpu as pltpu
from jax.sharding import PartitionSpec as P

F32 = jnp.float32
BF16 = jnp.bfloat16
VMEM = pl.BlockSpec(memory_space=pltpu.VMEM)
SMEM = pl.BlockSpec(memory_space=pltpu.SMEM)
LOG2E = 1.4426950408889634
AXES = ("img", "txt")
NN = (((1,), (0,)), ((), ()))
NT = (((1,), (1,)), ((), ()))
TN = (((0,), (0,)), ((), ()))
STEPS = (0, -1, 1, 2)
TAIL = 16


def params(mib):
    return pltpu.CompilerParams(vmem_limit_bytes=mib * 2**20)


def cost(flops, size):
    return pl.CostEstimate(flops=flops, bytes_accessed=size, transcendentals=0)


def moves():
    def perm(f):
        pairs = []
        for x in range(4):
            for y in range(4):
                for hi in range(2):
                    for lo in range(2):
                        for c in range(2):
                            a = (x, y, hi, lo, c)
                            number = lambda x, y, hi, lo, c: (x * 2 + lo) * 16 + (y * 2 + hi) * 2 + c
                            pairs.append((number(*a), number(*f(*a))))
        return pairs

    out = {}
    for s in (1, -1, 2):
        out["y", s] = perm(lambda x, y, hi, lo, c: (x, (y + s) % 4, hi, lo, c))
        out["x", s] = perm(lambda x, y, hi, lo, c: ((x + s) % 4, y, hi, lo, c))
    out["hi"] = perm(lambda x, y, hi, lo, c: (x, y, 1 - hi, lo, c))
    out["lo"] = perm(lambda x, y, hi, lo, c: (x, y, hi, 1 - lo, c))
    out["core"] = perm(lambda x, y, hi, lo, c: (x, y, hi, lo, 1 - c))
    return out


MOVES = moves()


def send(value, move):
    return lax.ppermute(value, AXES, MOVES[move])


def after(value, *others):
    return lax.optimization_barrier((value, *others))[0]


def split3(value, rounded=lambda v: v.astype(BF16).astype(F32)):
    high = rounded(value)
    middle = rounded(value - high)
    return high, middle, rounded(value - high - middle)


def unit_kernel(image, pairs, out, inverse):
    value = image[...].astype(F32)
    scale = 1.0 / jnp.sqrt(jnp.sum(value * value, axis=1, keepdims=True) + 1e-06)
    inverse[...] = scale
    unit = (value * scale).astype(BF16)
    rows, width = unit.shape
    half = rows // 2
    out[:half, :] = unit[:half]
    out[half + TAIL :, :] = unit[half:]
    index = pairs[...]
    kind = lax.broadcasted_iota(jnp.int32, (TAIL, rows), 0)
    part = jnp.where(kind == 0, index >> 8, jnp.where(kind == 1, index & 255, 0))
    out[half : half + TAIL, :] = jnp.zeros((TAIL, width), BF16)
    out[half : half + TAIL, :rows] = part.astype(F32).astype(BF16)


def image_units(image, pairs):
    rows, width = image.shape
    pairs = pairs[None]
    return pl.pallas_call(
        unit_kernel,
        out_shape=[
            jax.ShapeDtypeStruct((rows + TAIL, width), BF16),
            jax.ShapeDtypeStruct((rows, 1), F32),
        ],
        in_specs=[VMEM] * 2,
        out_specs=[VMEM] * 2,
        compiler_params=params(8),
        cost_estimate=cost(0, 4 * rows * width),
        name="image_units",
    )(image, pairs)


def text_kernel(place, *refs):
    pieces, (unit, raw, inverse) = refs[:-3], refs[-3:]
    total = None
    for piece in pieces:
        value = piece[...].astype(F32)
        part = jnp.sum(value * value, axis=0, keepdims=True)
        total = part if total is None else total + part
    scale = 1.0 / jnp.sqrt(total + 1e-06)
    inverse[...] = scale
    depth = unit.shape[0] // 8
    block = 0
    for piece in pieces:
        for start in range(0, piece.shape[0], depth):
            rows = pl.ds(pl.multiple_of(place[block] * depth, 16), depth)
            value = piece[start : start + depth, :]
            raw[rows, :] = value
            unit[rows, :] = (value.astype(F32) * scale).astype(BF16)
            block += 1


def text_units(place, pieces, depth):
    width = pieces[0].shape[1]
    whole = jax.ShapeDtypeStruct((8 * depth, width), BF16)
    return pl.pallas_call(
        text_kernel,
        out_shape=[whole, whole, jax.ShapeDtypeStruct((1, width), F32)],
        in_specs=[SMEM] + [VMEM] * len(pieces),
        out_specs=[VMEM] * 3,
        compiler_params=params(12),
        cost_estimate=cost(40_000_000_000, 32 * depth * width),
        name="text_units",
    )(place, *pieces)


def weight_kernel(rows, scalars, first_text, *refs):
    pieces, text, (image, weight, other, tails) = refs[:-5], refs[-5], refs[-4:]
    half = rows // 2
    halves = []
    for piece in pieces:
        done = 0
        while done < piece.shape[0]:
            halves.append((piece, done))
            done += half + TAIL if len(halves) % 2 else half
    for block in range(8):
        (a, i), (b, j) = halves[2 * block : 2 * block + 2]
        at = block * rows
        image[at : at + half, :] = a[i : i + half, :]
        image[at + half : at + rows, :] = b[j : j + half, :]
        tails[block * TAIL : (block + 1) * TAIL, :] = a[i + half : i + half + TAIL, :rows]
    slope, shift = scalars[0], scalars[1]
    columns = text.shape[1]
    eye = lax.broadcasted_iota(jnp.int32, (rows, rows), 0) == lax.broadcasted_iota(
        jnp.int32, (rows, rows), 1
    )
    names = (lax.broadcasted_iota(jnp.int32, (rows, columns), 1) + first_text[0]).astype(F32)

    def step(number, carry):
        for k in range(4):
            block = number * 4 + k
            mine = pl.ds(pl.multiple_of(block * rows, 16), rows)
            tail = tails[pl.ds(pl.multiple_of(block * TAIL, 16), TAIL), :].astype(F32)
            product = lax.dot_general(
                image[mine, :], text[...], NN, preferred_element_type=F32
            )
            chance = 1.0 / (1.0 + jnp.exp2(product * slope + shift))
            match = jnp.sum(
                jnp.where(eye, tail[0:1] * 256.0 + tail[1:2], 0.0), axis=1, keepdims=True
            )
            weight[mine, :] = (chance - jnp.where(match == names, 1.0, 0.0)).astype(BF16)
        return carry

    lax.fori_loop(0, 8 // 4, step, 0)
    other[...] = weight[4 * rows :, :]


def weights(scalars, first_text, pieces, rows, text):
    width, columns = text.shape
    count = 8 * rows
    return pl.pallas_call(
        lambda *refs: weight_kernel(rows, *refs),
        out_shape=[
            jax.ShapeDtypeStruct((count, width), BF16),
            jax.ShapeDtypeStruct((count, columns), BF16),
            jax.ShapeDtypeStruct((count // 2, columns), BF16),
        ],
        in_specs=[SMEM, SMEM] + [VMEM] * (len(pieces) + 1),
        out_specs=[VMEM] * 3,
        scratch_shapes=[pltpu.VMEM((8 * TAIL, rows), BF16)],
        compiler_params=params(12),
        cost_estimate=cost(8_000_000_000, 2 * count * (width + columns)),
        name="weights",
    )(scalars, first_text, *pieces, text)


def text_back_kernel(place, image_a, weight_a, image_b, weight_b, raw, *refs):
    outs, back = refs[:8], refs[8]
    width, columns = back.shape
    block = 384
    dots = jnp.zeros((1, columns), F32)
    for f in range(0, width, block):
        part = lax.dot_general(
            image_a[:, f : f + block], weight_a[...], TN, preferred_element_type=F32
        ) + lax.dot_general(
            image_b[:, f : f + block], weight_b[...], TN, preferred_element_type=F32
        )
        back[f : f + block, :] = part
        dots += jnp.sum(part * raw[f : f + block, :].astype(F32), axis=0, keepdims=True)
    tail = split3(dots)
    empty = jnp.zeros((1, columns), F32)
    depth = width // 8
    for i in range(4):
        for h in range(2):
            out = outs[2 * i + h]
            start = pl.multiple_of(place[2 * i + h] * depth, 16)
            out[:depth, :] = back[pl.ds(start, depth), :].astype(out.dtype)
        spread = [empty] * 3 * i + list(tail) + [empty] * (TAIL - 3 * i - 3)
        out[depth:, :] = jnp.concatenate(spread, 0).astype(out.dtype)


def text_terms(place, image_a, weight_a, image_b, weight_b, raw):
    count, width = image_a.shape
    columns = weight_a.shape[1]
    return pl.pallas_call(
        text_back_kernel,
        out_shape=[
            jax.ShapeDtypeStruct((width // 8 + h * TAIL, columns), BF16 if i else F32)
            for i in range(4)
            for h in range(2)
        ],
        in_specs=[SMEM] + [VMEM] * 5,
        out_specs=[VMEM] * 8,
        scratch_shapes=[pltpu.VMEM((width, columns), F32)],
        compiler_params=params(16),
        cost_estimate=cost(4 * count * width * columns, 4 * count * columns),
        name="text_terms",
    )(place, image_a, weight_a, image_b, weight_b, raw)


def image_back_kernel(rows, own_a, got_a, own_b, got_b, text, text_got, *outs):
    for start in (2, 0):
        block = slice(start * rows, (start + 2) * rows)
        for h, (own, got) in enumerate(((own_a, got_a), (own_b, got_b))):
            back = lax.dot_general(
                own[block, :], text[...], NT, preferred_element_type=F32
            ) + lax.dot_general(got[block, :], text_got[...], NT, preferred_element_type=F32)
            for k in range(2):
                out = outs[2 * (start + k) + h]
                out[...] = back[k * rows : (k + 1) * rows].astype(out.dtype)


def image_terms(rows, own_a, got_a, own_b, got_b, text, text_got):
    width, columns = text.shape
    return pl.pallas_call(
        lambda *refs: image_back_kernel(rows, *refs),
        out_shape=[jax.ShapeDtypeStruct((rows, width), F32 if i < 2 else BF16) for i in range(8)],
        in_specs=[VMEM] * 6,
        out_specs=[VMEM] * 8,
        compiler_params=params(16),
        cost_estimate=cost(10_000_000_000, 8 * width * columns),
        name="image_terms",
    )(own_a, got_a, own_b, got_b, text, text_got)


def add_kernel(at, value, more, out):
    rows = more.shape[0]
    for start in range(0, value.shape[0], 16):
        block = slice(start, start + 16)
        if at <= start < at + rows:
            total = value[block, :].astype(F32) + more[start - at : start - at + 16, :].astype(F32)
            out[block, :] = total.astype(BF16)
        else:
            out[block, :] = value[block, :]


def add_rows(value, more, at):
    return pl.pallas_call(
        lambda *refs: add_kernel(at, *refs),
        out_shape=jax.ShapeDtypeStruct(value.shape, BF16),
        in_specs=[VMEM] * 2,
        out_specs=VMEM,
        compiler_params=params(8),
        cost_estimate=cost(5_000_000_000, 6 * value.size),
        name="add_rows",
    )(value, more)


def hold_kernel(value, *refs):
    refs[-1][...] = value[...]


def hold(value, *others):
    return pl.pallas_call(
        hold_kernel,
        out_shape=jax.ShapeDtypeStruct(value.shape, value.dtype),
        in_specs=[VMEM] + [pl.BlockSpec(memory_space=pl.ANY)] * len(others),
        out_specs=VMEM,
        compiler_params=params(4),
        cost_estimate=cost(20_000_000_000, 0),
        name="hold",
    )(value, *others)


def add_three_kernel(own, ahead, back, out):
    out[...] = (own[...] + ahead[...].astype(F32) + back[...].astype(F32)).astype(BF16)


def add_three(own, ahead, back):
    return pl.pallas_call(
        add_three_kernel,
        out_shape=jax.ShapeDtypeStruct(own.shape, BF16),
        in_specs=[VMEM] * 3,
        out_specs=VMEM,
        compiler_params=params(8),
        cost_estimate=cost(0, 10 * own.size),
        name="add_three",
    )(own, ahead, back)


def image_final_kernel(temper, own, ahead, back, given, image, inverse, out):
    total = own[...] + ahead[...].astype(F32) + back[...].astype(F32) + given[...].astype(F32)
    scale = inverse[...]
    unit = image[...].astype(F32) * scale
    dot = jnp.sum(unit * total, axis=1, keepdims=True)
    out[...] = (temper[0] * (total - unit * dot) * scale).astype(BF16)


def image_final(temper, own, ahead, back, given, image, inverse):
    return pl.pallas_call(
        image_final_kernel,
        out_shape=jax.ShapeDtypeStruct(image.shape, BF16),
        in_specs=[SMEM] + [VMEM] * 6,
        out_specs=VMEM,
        compiler_params=params(8),
        cost_estimate=cost(0, 16 * image.size),
        name="image_final",
    )(temper, own, ahead, back, given, image, inverse)


def text_final_kernel(temper, own, ahead, back, gave, given, raw, inverse, out):
    depth = raw.shape[0]
    scale = inverse[...]
    total = own[...] + ahead[...].astype(F32) + back[...].astype(F32)
    total += given[:depth, :].astype(F32)
    tails = gave[depth:, :].astype(F32) + given[depth:, :].astype(F32)
    dots = jnp.sum(tails, axis=0, keepdims=True) * scale
    unit = raw[...].astype(F32) * scale
    out[...] = (temper[0] * (total - unit * dots) * scale).astype(BF16)


def text_final(temper, own, ahead, back, gave, given, raw, inverse):
    return pl.pallas_call(
        text_final_kernel,
        out_shape=jax.ShapeDtypeStruct(raw.shape, BF16),
        in_specs=[SMEM] + [VMEM] * 7,
        out_specs=VMEM,
        compiler_params=params(8),
        cost_estimate=cost(0, 16 * raw.size),
        name="text_final",
    )(temper, own, ahead, back, gave, given, raw, inverse)


def local(image, text, pair_text, log_scale, bias):
    img, txt = lax.axis_index("img"), lax.axis_index("txt")
    x, lo = img // 2, img % 2
    place = jnp.stack([(x + s + 4) % 4 * 2 + (lo + h) % 2 for s in STEPS for h in range(2)])
    temper = jnp.exp(log_scale[0])
    scalars = jnp.stack([-LOG2E * temper, -LOG2E * bias[0]])
    first_text = (txt * text.shape[0])[None]
    depth, rows = text.shape[1], image.shape[0]

    own_text = text.T
    text_lo = send(own_text, "lo")
    text_a, text_b = send(own_text, ("x", 1)), send(own_text, ("x", -1))
    unit, image_inverse = image_units(image, pair_text)
    a, b = send(unit, ("y", 1)), send(unit, ("y", -1))
    unit_hi = send(hold(unit, text_lo), "hi")
    text_c, text_a = lax.optimization_barrier((text_lo, text_a))
    text_c = send(text_c, ("x", 1))
    text_d, text_b = lax.optimization_barrier((text_lo, text_b))
    text_d = send(text_d, ("x", -1))
    text_a2 = send(text_a, ("x", 1))
    cut = rows // 2 + TAIL
    a2, b2 = send(a[:cut], ("y", 1)), send(b[cut:], ("y", -1))
    c = send(unit_hi, ("y", 1))
    d, b = lax.optimization_barrier((unit_hi, b))
    d = send(d, ("y", -1))
    text_d2 = send(text_d, ("x", -1))
    c, d, text_c, text_d = lax.optimization_barrier((c, d, text_c, text_d))
    c2, d2 = send(c[:cut], ("y", 1)), send(d[cut:], ("y", -1))
    near, partner = [unit, a, b, a2, b2], [unit_hi, c, d, c2, d2]
    near.append(after(send(jnp.concatenate(near, 0), "core"), c2, d2))
    partner += [
        send(jnp.concatenate(partner[:3], 0), "core"),
        send(jnp.concatenate(partner[3:], 0), "core"),
    ]
    text_pieces = [own_text, text_lo, text_a, text_c, text_b, text_d, text_a2, text_d2]

    text_unit, text_raw, text_inverse = text_units(place, text_pieces, depth)
    image_a, weight_a, other_a = weights(scalars, first_text, near, rows, text_unit)
    got_a = send(other_a, "core")
    image_b, weight_b, other_b = weights(
        after(scalars, other_a), first_text, partner, rows, text_unit
    )
    got_b = send(other_b, "core")
    text_got = send(after(text_unit, other_b), "core")
    text_parts = text_terms(place, image_a, weight_a, image_b, weight_b, text_raw)
    got_b, *text_parts = lax.optimization_barrier((got_b, *text_parts))
    image_parts = image_terms(rows, weight_a, got_a, weight_b, got_b, text_unit, text_got)

    x_own, x_back, x_ahead, x_far = [text_parts[2 * i : 2 * i + 2] for i in range(4)]
    y_own, y_back, y_ahead, y_far = [image_parts[2 * i : 2 * i + 2] for i in range(4)]

    x_relay1, x_relay0 = send(x_far[1], ("x", -1)), send(x_far[0], ("x", 1))
    x_ahead1 = send(x_ahead[1], ("x", 1))
    y_relay1, y_relay0 = send(y_far[1], ("y", -1)), send(y_far[0], ("y", 1))
    x_back0, x_back1, x_ahead0, _ = lax.optimization_barrier((*x_back, x_ahead[0], y_own[0]))
    x_back1, x_ahead0 = lax.optimization_barrier((add_rows(x_back1, x_relay1, 0), x_ahead0))
    x_ahead0 = add_rows(x_ahead0, x_relay0, 0)
    x_ahead0, y_back0, y_back1, y_ahead0, y_ahead1 = lax.optimization_barrier(
        (x_ahead0, *y_back, *y_ahead)
    )
    x_back1, x_ahead0 = send(x_back1, ("x", -1)), send(x_ahead0, ("x", 1))
    y_back1 = add_rows(y_back1, y_relay1, 0)
    y_back1, y_ahead1, x_back0 = lax.optimization_barrier((y_back1, y_ahead1, x_back0))
    y_back1, y_ahead1 = send(y_back1, ("y", -1)), send(y_ahead1, ("y", 1))
    x_gave = add_three(x_own[1], x_ahead1, x_back1)
    x_given = send(x_gave, "lo")
    x_back0 = send(x_back0, ("x", -1))
    y_ahead0, y_back0 = lax.optimization_barrier((add_rows(y_ahead0, y_relay0, 0), y_back0))
    y_ahead0, y_back0 = send(y_ahead0, ("y", 1)), send(y_back0, ("y", -1))
    y_given = send(add_three(y_own[1], y_ahead1, y_back1), "hi")

    grad_text = text_final(
        temper[None], x_own[0], x_ahead0, x_back0, x_gave, x_given, own_text, text_inverse
    )
    y_given, grad_text = lax.optimization_barrier((y_given, grad_text))
    grad_image = image_final(
        temper[None], y_own[0], y_ahead0, y_back0, y_given, image, image_inverse
    )
    return grad_image, grad_text.T


def solution(mesh):
    in_specs = (P(("img", "txt"), None), P("txt", "img"), P(("img", "txt")), P(), P())
    out_specs = (P(("img", "txt"), None), P("txt", "img"))
    return jax.shard_map(local, mesh=mesh, in_specs=in_specs, out_specs=out_specs, check_vma=False)
```

```python
import jax
import jax.numpy as jnp
from jax import lax
from jax.experimental import pallas as pl
from jax.experimental.pallas import tpu as pltpu
from jax.sharding import PartitionSpec as P

F32 = jnp.float32
BF16 = jnp.bfloat16
VMEM = pl.BlockSpec(memory_space=pltpu.VMEM)
SMEM = pl.BlockSpec(memory_space=pltpu.SMEM)
LOG2E = 1.4426950408889634
AXES = ("img", "txt")
NN = (((1,), (0,)), ((), ()))
NT = (((1,), (1,)), ((), ()))
TN = (((0,), (0,)), ((), ()))
STEPS = (0, -1, 1, 2)
TAIL = 16


def params(mib):
    return pltpu.CompilerParams(vmem_limit_bytes=mib * 2**20)


def cost(flops, size):
    return pl.CostEstimate(flops=flops, bytes_accessed=size, transcendentals=0)


def moves():
    def perm(f):
        pairs = []
        for x in range(4):
            for y in range(4):
                for hi in range(2):
                    for lo in range(2):
                        for c in range(2):
                            a = (x, y, hi, lo, c)
                            number = lambda x, y, hi, lo, c: (x * 2 + lo) * 16 + (y * 2 + hi) * 2 + c
                            pairs.append((number(*a), number(*f(*a))))
        return pairs

    out = {}
    for s in (1, -1, 2):
        out["y", s] = perm(lambda x, y, hi, lo, c: (x, (y + s) % 4, hi, lo, c))
        out["x", s] = perm(lambda x, y, hi, lo, c: ((x + s) % 4, y, hi, lo, c))
    out["hi"] = perm(lambda x, y, hi, lo, c: (x, y, 1 - hi, lo, c))
    out["lo"] = perm(lambda x, y, hi, lo, c: (x, y, hi, 1 - lo, c))
    out["core"] = perm(lambda x, y, hi, lo, c: (x, y, hi, lo, 1 - c))
    return out


MOVES = moves()


def send(value, move):
    return lax.ppermute(value, AXES, MOVES[move])


def after(value, *others):
    return lax.optimization_barrier((value, *others))[0]


def split3(value, rounded=lambda v: v.astype(BF16).astype(F32)):
    high = rounded(value)
    middle = rounded(value - high)
    return high, middle, rounded(value - high - middle)


def unit_kernel(image, pairs, out, inverse):
    value = image[...].astype(F32)
    scale = 1.0 / jnp.sqrt(jnp.sum(value * value, axis=1, keepdims=True) + 1e-06)
    inverse[...] = scale
    unit = (value * scale).astype(BF16)
    rows, width = unit.shape
    half = rows // 2
    out[:half, :] = unit[:half]
    out[half + TAIL :, :] = unit[half:]
    index = pairs[...]
    kind = lax.broadcasted_iota(jnp.int32, (TAIL, rows), 0)
    part = jnp.where(kind == 0, index >> 8, jnp.where(kind == 1, index & 255, 0))
    out[half : half + TAIL, :] = jnp.zeros((TAIL, width), BF16)
    out[half : half + TAIL, :rows] = part.astype(F32).astype(BF16)


def image_units(image, pairs):
    rows, width = image.shape
    pairs = pairs[None]
    return pl.pallas_call(
        unit_kernel,
        out_shape=[
            jax.ShapeDtypeStruct((rows + TAIL, width), BF16),
            jax.ShapeDtypeStruct((rows, 1), F32),
        ],
        in_specs=[VMEM] * 2,
        out_specs=[VMEM] * 2,
        compiler_params=params(8),
        cost_estimate=cost(0, 4 * rows * width),
        name="image_units",
    )(image, pairs)


def text_kernel(place, *refs):
    pieces, (unit, raw, inverse) = refs[:-3], refs[-3:]
    total = None
    for piece in pieces:
        value = piece[...].astype(F32)
        part = jnp.sum(value * value, axis=0, keepdims=True)
        total = part if total is None else total + part
    scale = 1.0 / jnp.sqrt(total + 1e-06)
    inverse[...] = scale
    depth = unit.shape[0] // 8
    block = 0
    for piece in pieces:
        for start in range(0, piece.shape[0], depth):
            rows = pl.ds(pl.multiple_of(place[block] * depth, 16), depth)
            value = piece[start : start + depth, :]
            raw[rows, :] = value
            unit[rows, :] = (value.astype(F32) * scale).astype(BF16)
            block += 1


def text_units(place, pieces, depth):
    width = pieces[0].shape[1]
    whole = jax.ShapeDtypeStruct((8 * depth, width), BF16)
    return pl.pallas_call(
        text_kernel,
        out_shape=[whole, whole, jax.ShapeDtypeStruct((1, width), F32)],
        in_specs=[SMEM] + [VMEM] * len(pieces),
        out_specs=[VMEM] * 3,
        compiler_params=params(12),
        cost_estimate=cost(40_000_000_000, 32 * depth * width),
        name="text_units",
    )(place, *pieces)


def weight_kernel(rows, scalars, first_text, *refs):
    pieces, text, (image, weight, other, tails) = refs[:-5], refs[-5], refs[-4:]
    half = rows // 2
    halves = []
    for piece in pieces:
        done = 0
        while done < piece.shape[0]:
            halves.append((piece, done))
            done += half + TAIL if len(halves) % 2 else half
    for block in range(8):
        (a, i), (b, j) = halves[2 * block : 2 * block + 2]
        at = block * rows
        image[at : at + half, :] = a[i : i + half, :]
        image[at + half : at + rows, :] = b[j : j + half, :]
        tails[block * TAIL : (block + 1) * TAIL, :] = a[i + half : i + half + TAIL, :rows]
    slope, shift = scalars[0], scalars[1]
    columns = text.shape[1]
    eye = lax.broadcasted_iota(jnp.int32, (rows, rows), 0) == lax.broadcasted_iota(
        jnp.int32, (rows, rows), 1
    )
    names = (lax.broadcasted_iota(jnp.int32, (rows, columns), 1) + first_text[0]).astype(F32)

    def step(number, carry):
        for k in range(8):
            block = number * 8 + k
            mine = pl.ds(pl.multiple_of(block * rows, 16), rows)
            tail = tails[pl.ds(pl.multiple_of(block * TAIL, 16), TAIL), :].astype(F32)
            product = lax.dot_general(
                image[mine, :], text[...], NN, preferred_element_type=F32
            )
            chance = 1.0 / (1.0 + jnp.exp2(product * slope + shift))
            match = jnp.sum(
                jnp.where(eye, tail[0:1] * 256.0 + tail[1:2], 0.0), axis=1, keepdims=True
            )
            weight[mine, :] = (chance - jnp.where(match == names, 1.0, 0.0)).astype(BF16)
        return carry

    lax.fori_loop(0, 8 // 8, step, 0)
    other[...] = weight[4 * rows :, :]


def weights(scalars, first_text, pieces, rows, text):
    width, columns = text.shape
    count = 8 * rows
    return pl.pallas_call(
        lambda *refs: weight_kernel(rows, *refs),
        out_shape=[
            jax.ShapeDtypeStruct((count, width), BF16),
            jax.ShapeDtypeStruct((count, columns), BF16),
            jax.ShapeDtypeStruct((count // 2, columns), BF16),
        ],
        in_specs=[SMEM, SMEM] + [VMEM] * (len(pieces) + 1),
        out_specs=[VMEM] * 3,
        scratch_shapes=[pltpu.VMEM((8 * TAIL, rows), BF16)],
        compiler_params=params(12),
        cost_estimate=cost(8_000_000_000, 2 * count * (width + columns)),
        name="weights",
    )(scalars, first_text, *pieces, text)


def text_back_kernel(place, image_a, weight_a, image_b, weight_b, raw, *refs):
    outs, back = refs[:8], refs[8]
    width, columns = back.shape
    block = 384

    def step(number, dots):
        mine = pl.ds(pl.multiple_of(number * block, block), block)
        part = lax.dot_general(
            image_a[:, mine], weight_a[...], TN, preferred_element_type=F32
        ) + lax.dot_general(image_b[:, mine], weight_b[...], TN, preferred_element_type=F32)
        back[mine, :] = part
        return dots + jnp.sum(part * raw[mine, :].astype(F32), axis=0, keepdims=True)

    dots = lax.fori_loop(0, width // block, step, jnp.zeros((1, columns), F32))
    tail = split3(dots)
    empty = jnp.zeros((1, columns), F32)
    depth = width // 8
    for i in range(4):
        for h in range(2):
            out = outs[2 * i + h]
            start = pl.multiple_of(place[2 * i + h] * depth, 16)
            out[:depth, :] = back[pl.ds(start, depth), :].astype(out.dtype)
        spread = [empty] * 3 * i + list(tail) + [empty] * (TAIL - 3 * i - 3)
        out[depth:, :] = jnp.concatenate(spread, 0).astype(out.dtype)


def text_terms(place, image_a, weight_a, image_b, weight_b, raw):
    count, width = image_a.shape
    columns = weight_a.shape[1]
    return pl.pallas_call(
        text_back_kernel,
        out_shape=[
            jax.ShapeDtypeStruct((width // 8 + h * TAIL, columns), BF16 if i else F32)
            for i in range(4)
            for h in range(2)
        ],
        in_specs=[SMEM] + [VMEM] * 5,
        out_specs=[VMEM] * 8,
        scratch_shapes=[pltpu.VMEM((width, columns), F32)],
        compiler_params=params(16),
        cost_estimate=cost(4 * count * width * columns, 4 * count * columns),
        name="text_terms",
    )(place, image_a, weight_a, image_b, weight_b, raw)


def image_back_kernel(rows, own_a, got_a, own_b, got_b, text, text_got, *outs):
    for start in (2, 0):
        block = slice(start * rows, (start + 2) * rows)
        for h, (own, got) in enumerate(((own_a, got_a), (own_b, got_b))):
            back = lax.dot_general(
                own[block, :], text[...], NT, preferred_element_type=F32
            ) + lax.dot_general(got[block, :], text_got[...], NT, preferred_element_type=F32)
            for k in range(2):
                out = outs[2 * (start + k) + h]
                out[...] = back[k * rows : (k + 1) * rows].astype(out.dtype)


def image_terms(rows, own_a, got_a, own_b, got_b, text, text_got):
    width, columns = text.shape
    return pl.pallas_call(
        lambda *refs: image_back_kernel(rows, *refs),
        out_shape=[jax.ShapeDtypeStruct((rows, width), F32 if i < 2 else BF16) for i in range(8)],
        in_specs=[VMEM] * 6,
        out_specs=[VMEM] * 8,
        compiler_params=params(16),
        cost_estimate=cost(10_000_000_000, 8 * width * columns),
        name="image_terms",
    )(own_a, got_a, own_b, got_b, text, text_got)


def add_kernel(at, value, more, out):
    rows = more.shape[0]
    for start in range(0, value.shape[0], 16):
        block = slice(start, start + 16)
        if at <= start < at + rows:
            total = value[block, :].astype(F32) + more[start - at : start - at + 16, :].astype(F32)
            out[block, :] = total.astype(BF16)
        else:
            out[block, :] = value[block, :]


def add_rows(value, more, at):
    return pl.pallas_call(
        lambda *refs: add_kernel(at, *refs),
        out_shape=jax.ShapeDtypeStruct(value.shape, BF16),
        in_specs=[VMEM] * 2,
        out_specs=VMEM,
        compiler_params=params(8),
        cost_estimate=cost(5_000_000_000, 6 * value.size),
        name="add_rows",
    )(value, more)


def hold_kernel(value, *refs):
    refs[-1][...] = value[...]


def hold(value, *others):
    return pl.pallas_call(
        hold_kernel,
        out_shape=jax.ShapeDtypeStruct(value.shape, value.dtype),
        in_specs=[VMEM] + [pl.BlockSpec(memory_space=pl.ANY)] * len(others),
        out_specs=VMEM,
        compiler_params=params(4),
        cost_estimate=cost(20_000_000_000, 0),
        name="hold",
    )(value, *others)


def add_three_kernel(own, ahead, back, out):
    out[...] = (own[...] + ahead[...].astype(F32) + back[...].astype(F32)).astype(BF16)


def add_three(own, ahead, back):
    return pl.pallas_call(
        add_three_kernel,
        out_shape=jax.ShapeDtypeStruct(own.shape, BF16),
        in_specs=[VMEM] * 3,
        out_specs=VMEM,
        compiler_params=params(8),
        cost_estimate=cost(0, 10 * own.size),
        name="add_three",
    )(own, ahead, back)


def image_final_kernel(temper, own, ahead, back, given, image, inverse, out):
    total = own[...] + ahead[...].astype(F32) + back[...].astype(F32) + given[...].astype(F32)
    scale = inverse[...]
    unit = image[...].astype(F32) * scale
    dot = jnp.sum(unit * total, axis=1, keepdims=True)
    out[...] = (temper[0] * (total - unit * dot) * scale).astype(BF16)


def image_final(temper, own, ahead, back, given, image, inverse):
    return pl.pallas_call(
        image_final_kernel,
        out_shape=jax.ShapeDtypeStruct(image.shape, BF16),
        in_specs=[SMEM] + [VMEM] * 6,
        out_specs=VMEM,
        compiler_params=params(8),
        cost_estimate=cost(0, 16 * image.size),
        name="image_final",
    )(temper, own, ahead, back, given, image, inverse)


def text_final_kernel(temper, own, ahead, back, gave, given, raw, inverse, out):
    depth = raw.shape[0]
    scale = inverse[...]
    total = own[...] + ahead[...].astype(F32) + back[...].astype(F32)
    total += given[:depth, :].astype(F32)
    tails = gave[depth:, :].astype(F32) + given[depth:, :].astype(F32)
    dots = jnp.sum(tails, axis=0, keepdims=True) * scale
    unit = raw[...].astype(F32) * scale
    out[...] = (temper[0] * (total - unit * dots) * scale).astype(BF16)


def text_final(temper, own, ahead, back, gave, given, raw, inverse):
    return pl.pallas_call(
        text_final_kernel,
        out_shape=jax.ShapeDtypeStruct(raw.shape, BF16),
        in_specs=[SMEM] + [VMEM] * 7,
        out_specs=VMEM,
        compiler_params=params(8),
        cost_estimate=cost(0, 16 * raw.size),
        name="text_final",
    )(temper, own, ahead, back, gave, given, raw, inverse)


def local(image, text, pair_text, log_scale, bias):
    img, txt = lax.axis_index("img"), lax.axis_index("txt")
    x, lo = img // 2, img % 2
    place = jnp.stack([(x + s + 4) % 4 * 2 + (lo + h) % 2 for s in STEPS for h in range(2)])
    temper = jnp.exp(log_scale[0])
    scalars = jnp.stack([-LOG2E * temper, -LOG2E * bias[0]])
    first_text = (txt * text.shape[0])[None]
    depth, rows = text.shape[1], image.shape[0]

    own_text = text.T
    text_lo = send(own_text, "lo")
    text_a, text_b = send(own_text, ("x", 1)), send(own_text, ("x", -1))
    unit, image_inverse = image_units(image, pair_text)
    a, b = send(unit, ("y", 1)), send(unit, ("y", -1))
    unit_hi = send(hold(unit, text_lo), "hi")
    text_c, text_a = lax.optimization_barrier((text_lo, text_a))
    text_c = send(text_c, ("x", 1))
    text_d, text_b = lax.optimization_barrier((text_lo, text_b))
    text_d = send(text_d, ("x", -1))
    text_a2 = send(text_a, ("x", 1))
    cut = rows // 2 + TAIL
    a2, b2 = send(a[:cut], ("y", 1)), send(b[cut:], ("y", -1))
    c = send(unit_hi, ("y", 1))
    d, b = lax.optimization_barrier((unit_hi, b))
    d = send(d, ("y", -1))
    text_d2 = send(text_d, ("x", -1))
    c, d, text_c, text_d = lax.optimization_barrier((c, d, text_c, text_d))
    c2, d2 = send(c[:cut], ("y", 1)), send(d[cut:], ("y", -1))
    near, partner = [unit, a, b, a2, b2], [unit_hi, c, d, c2, d2]
    near.append(after(send(jnp.concatenate(near, 0), "core"), c2, d2))
    partner += [
        send(jnp.concatenate(partner[:3], 0), "core"),
        send(jnp.concatenate(partner[3:], 0), "core"),
    ]
    text_pieces = [own_text, text_lo, text_a, text_c, text_b, text_d, text_a2, text_d2]

    text_unit, text_raw, text_inverse = text_units(place, text_pieces, depth)
    image_a, weight_a, other_a = weights(scalars, first_text, near, rows, text_unit)
    got_a = send(other_a, "core")
    image_b, weight_b, other_b = weights(
        after(scalars, other_a), first_text, partner, rows, text_unit
    )
    got_b = send(other_b, "core")
    text_got = send(after(text_unit, other_b), "core")
    text_parts = text_terms(place, image_a, weight_a, image_b, weight_b, text_raw)
    got_b, *text_parts = lax.optimization_barrier((got_b, *text_parts))
    image_parts = image_terms(rows, weight_a, got_a, weight_b, got_b, text_unit, text_got)

    x_own, x_back, x_ahead, x_far = [text_parts[2 * i : 2 * i + 2] for i in range(4)]
    y_own, y_back, y_ahead, y_far = [image_parts[2 * i : 2 * i + 2] for i in range(4)]

    x_relay1, x_relay0 = send(x_far[1], ("x", -1)), send(x_far[0], ("x", 1))
    x_ahead1 = send(x_ahead[1], ("x", 1))
    y_relay1, y_relay0 = send(y_far[1], ("y", -1)), send(y_far[0], ("y", 1))
    x_back0, x_back1, x_ahead0, _ = lax.optimization_barrier((*x_back, x_ahead[0], y_own[0]))
    x_back1, x_ahead0 = add_rows(x_back1, x_relay1, 0), add_rows(x_ahead0, x_relay0, 0)
    x_ahead0, y_back0, y_back1, y_ahead0, y_ahead1 = lax.optimization_barrier(
        (x_ahead0, *y_back, *y_ahead)
    )
    x_back1, x_ahead0 = send(x_back1, ("x", -1)), send(x_ahead0, ("x", 1))
    y_back1 = add_rows(y_back1, y_relay1, 0)
    y_back1, y_ahead1, x_back0 = lax.optimization_barrier((y_back1, y_ahead1, x_back0))
    y_back1, y_ahead1 = send(y_back1, ("y", -1)), send(y_ahead1, ("y", 1))
    x_gave = add_three(x_own[1], x_ahead1, x_back1)
    x_given = send(x_gave, "lo")
    x_back0 = send(x_back0, ("x", -1))
    y_ahead0, y_back0 = lax.optimization_barrier((add_rows(y_ahead0, y_relay0, 0), y_back0))
    y_ahead0, y_back0 = send(y_ahead0, ("y", 1)), send(y_back0, ("y", -1))
    y_given = send(add_three(y_own[1], y_ahead1, y_back1), "hi")

    grad_text = text_final(
        temper[None], x_own[0], x_ahead0, x_back0, x_gave, x_given, own_text, text_inverse
    )
    y_given, grad_text = lax.optimization_barrier((y_given, grad_text))
    grad_image = image_final(
        temper[None], y_own[0], y_ahead0, y_back0, y_given, image, image_inverse
    )
    return grad_image, grad_text.T


def solution(mesh):
    in_specs = (P(("img", "txt"), None), P("txt", "img"), P(("img", "txt")), P(), P())
    out_specs = (P(("img", "txt"), None), P("txt", "img"))
    return jax.shard_map(local, mesh=mesh, in_specs=in_specs, out_specs=out_specs, check_vma=False)
```
